32 devices in a mesh: dom: 8 (over z, y), tile: 4 (over x, core).
Axes of the slice: x: 2, y: 2, z: 4, core: 2. Of those that a mesh axis runs over, the one named last changes fastest.
Arguments:
- tile_latent: bfloat16 [4096, 512], P(('dom', 'tile')), may hold values from -6 to 6
- relay_pick: int32 [32, 128], P(('dom', 'tile')), may hold values from 0 to 127, as said below
- relay_from: int32 [4096], P(('dom', 'tile')), may hold values from 0 to 255, as said below
- cut_pick: int32 [32, 32], P(('dom', 'tile')), may hold values from 0 to 127, as said below
- edge_latent: bfloat16 [24576, 512], P(('dom', 'tile')), may hold values from -6 to 6
- edge_sender: int32 [24576], P(('dom', 'tile')), may hold values from 0 to 543, as said below
- edge_receiver: int32 [24576], P(('dom', 'tile')), may hold values from 0 to 127, as said below
- edge_in: bfloat16 [1536, 512], replicated, may hold values from -0.15625 to 0.15625
- edge_out: bfloat16 [512, 512], replicated
- node_in: bfloat16 [1024, 512], replicated, may hold values from -0.1875 to 0.1875
- node_out: bfloat16 [512, 512], replicated
- node_cot: bfloat16 [4096, 512], P(('dom', 'tile')), may hold values from -6 to 6
- edge_cot: bfloat16 [24576, 512], P(('dom', 'tile')), may hold values from -6 to 6
Outputs:
- node_update: bfloat16 [4096, 512], P(('dom', 'tile'))
- edge_update: bfloat16 [24576, 512], P(('dom', 'tile'))
- latent_grad: bfloat16 [4096, 512], P(('dom', 'tile'))
- edge_grad: bfloat16 [24576, 512], P(('dom', 'tile'))
- weight_grad: float32 [3584, 512], P('dom', 'tile')
The draws below stay inside these ranges and needn't reach their ends.
Inputs may be any that keep to these rules, and one draw needn't show every extreme that they name: `relay_pick`: slot j of the block for partition q on device (p, t) carries a row when j is under that pair's count; the counts depend on the partition offset q - p and are 16 or half of it, zero for q = p; the other slots name rows that no one reads. No tile row goes out twice, and the rows that go out nowhere stay on their device. `relay_from`: each device's block names 128 distinct places: its own staying tile rows (below 128) or received slots that carry a row, 128 + s * 16 + j for slot j from partition s. `cut_pick`: distinct rows within a device. `edge_sender`: below 512: a node of the device's own partition; above: a halo slot, first the 16 from the lower partition, then the 16 from the upper. `edge_receiver`: not falling within a device.
All inputs are finite; a program needn't handle non-finite values.
Results may differ from the reference program's by a relative error of at most 0.013.
Values may be sent and summed in bfloat16 or wider, within the bound.
No kernel may reach another device: no remote copies, remote signals or barrier semaphores. Data moves between devices by JAX's collectives and lax.ppermute only.
A program may use at most 128 MiB of HBM per device.

```python
import math
import jax
import jax.numpy as jnp
from jax import lax

H = 512
NODE_DEV = 128
EDGE_DEV = 768
RELAY_CAP = 16
HALO_CAP = 16
NODES = 4096
EDGES = 24576
N_DOM = 8
N_TILE = 4


def relay_plan(key):
    device_count = N_DOM * N_TILE
    span = NODE_DEV + N_DOM * RELAY_CAP
    row_order = jax.vmap(lambda subkey: jax.random.permutation(subkey, NODE_DEV))(jax.random.split(jax.random.fold_in(key, 101), device_count)).astype(jnp.int32).reshape(N_DOM, N_TILE, NODE_DEV)
    ranking = jax.vmap(lambda subkey: jax.random.permutation(subkey, N_DOM - 1))(jax.random.split(jax.random.fold_in(key, 102), N_TILE)).astype(jnp.int32)
    counts = jnp.where(ranking % 2 == 0, RELAY_CAP, RELAY_CAP // 2).astype(jnp.int32)
    counts = jnp.concatenate([jnp.zeros((N_TILE, 1), jnp.int32), counts], 1)
    starts = jnp.cumsum(counts, 1) - counts
    staying = NODE_DEV - jnp.sum(counts, 1)
    source = jnp.arange(N_DOM, dtype=jnp.int32)[:, None, None, None]
    column = jnp.arange(N_TILE, dtype=jnp.int32)[None, :, None, None]
    target = jnp.arange(N_DOM, dtype=jnp.int32)[None, None, :, None]
    slot_index = jnp.arange(RELAY_CAP, dtype=jnp.int32)[None, None, None, :]
    offset = (target - source) % N_DOM
    is_live = slot_index < counts[column, offset]
    position = jnp.clip(staying[column] + starts[column, offset] + slot_index, 0, NODE_DEV - 1)
    chosen = jnp.where(is_live, position, slot_index % NODE_DEV)
    chosen = jnp.broadcast_to(chosen, (N_DOM, N_TILE, N_DOM, RELAY_CAP)).reshape(N_DOM, N_TILE, N_DOM * RELAY_CAP)
    pick_list = jnp.take_along_axis(row_order, chosen, axis=2).reshape(device_count, N_DOM * RELAY_CAP)
    inverse = jnp.argsort(row_order, axis=2).astype(jnp.int32)
    own_valid = inverse < staying[None, :, None]
    got = slot_index < counts[column, (source - target) % N_DOM]
    got = jnp.broadcast_to(got, (N_DOM, N_TILE, N_DOM, RELAY_CAP)).reshape(N_DOM, N_TILE, N_DOM * RELAY_CAP)
    is_valid = jnp.concatenate([jnp.broadcast_to(own_valid, (N_DOM, N_TILE, NODE_DEV)), got], 2)
    shuffle = jax.vmap(lambda subkey: jax.random.permutation(subkey, span))(jax.random.split(jax.random.fold_in(key, 103), device_count)).astype(jnp.int32).reshape(N_DOM, N_TILE, span)
    sort_score = jnp.where(is_valid, shuffle, shuffle + span)
    from_list = jnp.argsort(sort_score, axis=2)[:, :, :NODE_DEV].astype(jnp.int32)
    return (pick_list, from_list.reshape(-1))


def draw_relay_pick(key, part):
    plan = relay_plan(key)
    return plan[0]


def draw_relay_from(key, part):
    plan = relay_plan(key)
    return plan[1]


def draw_cut_pick(key, part):
    key = jax.random.fold_in(key, 3)
    subkeys = jax.random.split(key, N_DOM * N_TILE)
    return jax.vmap(lambda subkey: jax.random.permutation(subkey, NODE_DEV)[:2 * HALO_CAP])(subkeys).astype(jnp.int32)


def draw_edge_receiver(key, part):
    key = jax.random.fold_in(key, 5)
    drawn = jax.random.randint(key, (N_DOM * N_TILE, EDGE_DEV), 0, NODE_DEV, dtype=jnp.int32)
    return jnp.sort(drawn, axis=1).reshape(-1).astype(jnp.int32)


def draw_edge_sender(key, part):
    key = jax.random.fold_in(key, 7)
    subkeys = jax.random.split(key, 6)
    device_count = N_DOM * N_TILE
    part_rows = N_TILE * NODE_DEV
    used_rows = jax.random.randint(subkeys[0], (N_DOM * N_TILE * 2,), HALO_CAP // 2, HALO_CAP + 1, dtype=jnp.int32)
    forced = jax.random.randint(subkeys[1], (), 0, N_DOM * N_TILE * 2, dtype=jnp.int32)
    used_rows = used_rows.at[forced].set(HALO_CAP).reshape(N_DOM, N_TILE, 2)
    from_lower = jnp.roll(used_rows[:, :, 1], 1, axis=0).reshape(device_count, 1)
    from_upper = jnp.roll(used_rows[:, :, 0], -1, axis=0).reshape(device_count, 1)
    side_pick = jax.random.randint(subkeys[2], (device_count, EDGE_DEV), 0, 2, dtype=jnp.int32)
    slot_limit = jnp.where(side_pick == 0, from_lower, from_upper)
    slot_index = jax.random.randint(subkeys[3], (device_count, EDGE_DEV), 0, slot_limit, dtype=jnp.int32)
    is_cut = jax.random.randint(subkeys[4], (device_count, EDGE_DEV), 0, 4, dtype=jnp.int32) == 0
    inner_rows = jax.random.randint(subkeys[5], (device_count, EDGE_DEV), 0, part_rows, dtype=jnp.int32)
    return jnp.where(is_cut, part_rows + side_pick * HALO_CAP + slot_index, inner_rows).reshape(-1).astype(jnp.int32)


def draw_edge_out(key, part):
    key = jax.random.fold_in(key, 11)
    subkeys = jax.random.split(key, 2)
    base_vals = jax.random.normal(subkeys[0], (H, H), jnp.float32)
    col_scale = jnp.exp(jax.random.uniform(subkeys[1], (1, H), jnp.float32, math.log(0.3), math.log(3.0)))
    return (base_vals * col_scale * H ** (-0.5)).astype(jnp.bfloat16)


def draw_node_out(key, part):
    key = jax.random.fold_in(key, 13)
    subkeys = jax.random.split(key, 2)
    base_vals = jax.random.normal(subkeys[0], (H, H), jnp.float32)
    col_scale = jnp.exp(jax.random.uniform(subkeys[1], (1, H), jnp.float32, math.log(0.3), math.log(3.0)))
    return (base_vals * col_scale * H ** (-0.5)).astype(jnp.bfloat16)


def shard_levels(rng, dims, cuts, smallest, high):
    gain = 1.0
    for axis_at, parts in cuts:
        draws = jax.random.uniform(jax.random.fold_in(jax.random.fold_in(rng, 6), axis_at), (parts,), jnp.float32, smallest / len(cuts), high / len(cuts))
        gain = gain * jnp.repeat(jnp.exp(draws), dims[axis_at] // parts).reshape((-1,) + (1,) * (len(dims) - 1 - axis_at))
    return gain


def noise(stream_key, shape, width, bound, pieces=(), held_as=jnp.bfloat16):
    gain = shard_levels(stream_key, shape, pieces, -0.22, 0.18) if pieces else 1.0
    result = jax.random.normal(stream_key, shape, jnp.float32) * width * gain
    return jnp.minimum(jnp.maximum(result, -bound), bound).astype(held_as)


def setup_inputs(seed: int = 0) -> dict:
    keys = jax.random.split(jax.random.key(seed), 14)
    return {
        "tile_latent": noise(keys[0], (NODES, H), 1.0, 6.0, ((0, 32),)),
        "relay_pick": draw_relay_pick(jax.random.fold_in(keys[13], 71), 0),
        "relay_from": draw_relay_from(jax.random.fold_in(keys[13], 71), 0),
        "cut_pick": draw_cut_pick(jax.random.fold_in(keys[13], 71), 0),
        "edge_latent": noise(keys[4], (EDGES, H), 1.0, 6.0, ((0, 32),)),
        "edge_sender": draw_edge_sender(jax.random.fold_in(keys[13], 71), 0),
        "edge_receiver": draw_edge_receiver(jax.random.fold_in(keys[13], 71), 0),
        "edge_in": noise(keys[7], (3 * H, H), (3 * H) ** -0.5, 0.15625),
        "edge_out": draw_edge_out(jax.random.fold_in(keys[13], 71), 0),
        "node_in": noise(keys[9], (2 * H, H), (2 * H) ** -0.5, 0.1875),
        "node_out": draw_node_out(jax.random.fold_in(keys[13], 71), 0),
        "node_cot": noise(keys[11], (NODES, H), 1.0, 6.0, ((0, 32),)),
        "edge_cot": noise(keys[12], (EDGES, H), 1.0, 6.0, ((0, 32),)),
    }


EPSILON = 1e-05

def layer_norm(values):
    center = values - lax.optimization_barrier(jnp.mean(values, -1, keepdims=True))
    inverse = lax.rsqrt(lax.optimization_barrier(jnp.mean(center * center, -1, keepdims=True)) + EPSILON)
    return (center * inverse, inverse)

def norm_grad(normed, inverse, upstream):
    mean_up = lax.optimization_barrier(jnp.mean(upstream, -1, keepdims=True))
    mean_cross = lax.optimization_barrier(jnp.mean(upstream * normed, -1, keepdims=True))
    return inverse * (upstream - mean_up - normed * mean_cross)

def silu_grad(values):
    sigmoid = jax.nn.sigmoid(values)
    return sigmoid * (1.0 + values * (1.0 - sigmoid))

def flat_dot(left_mat, right_mat):
    return jnp.dot(left_mat, right_mat, preferred_element_type=jnp.float32)

def inner_dot(left_mat, right_mat):
    return lax.dot_general(left_mat, right_mat, (((0,), (0,)), ((), ())), preferred_element_type=jnp.float32)

def outer_dot(left_mat, right_mat):
    return lax.dot_general(left_mat, right_mat, (((1,), (1,)), ((), ())), preferred_element_type=jnp.float32)

def local_block(latent, row_table, edge_lat, senders, receivers, edge_in, edge_out, node_in, node_out, node_grad_in, edge_grad_in):
    feat_dim = edge_out.shape[0]
    node_count = latent.shape[0]
    w_edge = edge_in[:feat_dim]
    w_send = edge_in[feat_dim:2 * feat_dim]
    w_recv = edge_in[2 * feat_dim:]
    w_node = node_in[:feat_dim]
    w_agg = node_in[feat_dim:]
    send_rows = jnp.take(row_table, senders, axis=0)
    recv_rows = jnp.take(latent, receivers, axis=0)
    recv_proj = flat_dot(latent, w_recv)
    edge_pre = flat_dot(edge_lat, w_edge) + flat_dot(send_rows, w_send) + jnp.take(recv_proj, receivers, axis=0)
    edge_act = jax.nn.silu(edge_pre).astype(jnp.bfloat16)
    edge_lin = flat_dot(edge_act, edge_out)
    edge_normed, edge_inv = layer_norm(edge_lin)
    edge_new = (edge_lat.astype(jnp.float32) + edge_normed).astype(jnp.bfloat16)
    incidence = (receivers[:, None] == jnp.arange(node_count, dtype=jnp.int32)[None, :]).astype(jnp.bfloat16)
    aggregate = inner_dot(incidence, edge_new).astype(jnp.bfloat16)
    node_pre = flat_dot(latent, w_node) + flat_dot(aggregate, w_agg)
    node_act = jax.nn.silu(node_pre).astype(jnp.bfloat16)
    node_lin = flat_dot(node_act, node_out)
    node_normed, node_inv = layer_norm(node_lin)
    node_new = (latent.astype(jnp.float32) + node_normed).astype(jnp.bfloat16)
    node_upstream = node_grad_in.astype(jnp.float32)
    node_lin_grad = norm_grad(node_normed, node_inv, node_upstream).astype(jnp.bfloat16)
    grad_node_out = inner_dot(node_act, node_lin_grad)
    node_pre_grad = (outer_dot(node_lin_grad, node_out) * silu_grad(node_pre)).astype(jnp.bfloat16)
    grad_node_in = jnp.concatenate([inner_dot(latent, node_pre_grad), inner_dot(aggregate, node_pre_grad)], 0)
    node_direct = node_upstream + outer_dot(node_pre_grad, w_node)
    agg_grad = outer_dot(node_pre_grad, w_agg)
    edge_up = edge_grad_in.astype(jnp.float32) + jnp.take(agg_grad, receivers, axis=0)
    edge_lin_grad = norm_grad(edge_normed, edge_inv, edge_up).astype(jnp.bfloat16)
    grad_edge_out = inner_dot(edge_act, edge_lin_grad)
    edge_pre_grad = (outer_dot(edge_lin_grad, edge_out) * silu_grad(edge_pre)).astype(jnp.bfloat16)
    edge_grad = (edge_up + outer_dot(edge_pre_grad, w_edge)).astype(jnp.bfloat16)
    recv_grad = jax.ops.segment_sum(outer_dot(edge_pre_grad, w_recv), receivers, node_count)
    node_local = node_direct + recv_grad
    table_grad = jax.ops.segment_sum(outer_dot(edge_pre_grad, w_send), senders, row_table.shape[0])
    grad_edge_in = jnp.concatenate([inner_dot(edge_lat, edge_pre_grad), inner_dot(send_rows, edge_pre_grad), inner_dot(recv_rows, edge_pre_grad)], 0)
    weight_grad = jnp.concatenate([grad_edge_in, grad_edge_out, grad_node_in, grad_node_out], 0)
    return (node_new, edge_new, edge_grad, node_local, table_grad, weight_grad)

def reference(tile_latent, relay_pick, relay_from, cut_pick, edge_latent, edge_sender, edge_receiver, edge_in, edge_out, node_in, node_out, node_cot, edge_cot):
    feat_dim = H
    device_count = N_DOM * N_TILE
    part_count = N_TILE * NODE_DEV
    tile_grid = tile_latent.reshape(N_DOM, N_TILE, NODE_DEV, feat_dim)
    pick_list = relay_pick.reshape(N_DOM, N_TILE, N_DOM * RELAY_CAP)
    outgoing = jnp.take_along_axis(tile_grid, pick_list[..., None], axis=2).reshape(N_DOM, N_TILE, N_DOM, RELAY_CAP, feat_dim)
    incoming = jnp.transpose(outgoing, (2, 1, 0, 3, 4)).reshape(N_DOM, N_TILE, N_DOM * RELAY_CAP, feat_dim)
    pooled = jnp.concatenate([tile_grid, incoming], 2)
    places = relay_from.reshape(N_DOM, N_TILE, NODE_DEV)
    latent = jnp.take_along_axis(pooled, places[..., None], axis=2)
    cut_lists = cut_pick.reshape(N_DOM, N_TILE, 2 * HALO_CAP)
    cut_rows = jnp.take_along_axis(latent, cut_lists[..., None], axis=2).reshape(N_DOM, N_TILE, 2, HALO_CAP, feat_dim)
    from_lower = jnp.roll(cut_rows[:, :, 1], 1, axis=0)
    from_upper = jnp.roll(cut_rows[:, :, 0], -1, axis=0)
    partition = jnp.broadcast_to(latent.reshape(N_DOM, 1, part_count, feat_dim), (N_DOM, N_TILE, part_count, feat_dim))
    row_table = jnp.concatenate([partition, from_lower, from_upper], 2)
    stacked = (latent.reshape(device_count, NODE_DEV, feat_dim), row_table.reshape(device_count, part_count + 2 * HALO_CAP, feat_dim), edge_latent.reshape(device_count, EDGE_DEV, feat_dim), edge_sender.reshape(device_count, EDGE_DEV), edge_receiver.reshape(device_count, EDGE_DEV), node_cot.reshape(device_count, NODE_DEV, feat_dim), edge_cot.reshape(device_count, EDGE_DEV, feat_dim))

    def device_step(grad_total, device_item):
        local_out = local_block(device_item[0], device_item[1], device_item[2], device_item[3], device_item[4], edge_in, edge_out, node_in, node_out, device_item[5], device_item[6])
        return (grad_total + local_out[5], local_out[:5])
    grad_total, results = lax.scan(device_step, jnp.zeros((7 * feat_dim, feat_dim), jnp.float32), stacked)
    node_new, edge_new, edge_grad, node_local, table_grad = results
    part_grad = lax.optimization_barrier(jnp.sum(table_grad[:, :part_count].reshape(N_DOM, N_TILE, N_TILE, NODE_DEV, feat_dim), axis=1))
    lower_grad = table_grad[:, part_count:part_count + HALO_CAP].reshape(N_DOM, N_TILE, HALO_CAP, feat_dim)
    upper_grad = table_grad[:, part_count + HALO_CAP:].reshape(N_DOM, N_TILE, HALO_CAP, feat_dim)
    back_lower = jnp.roll(upper_grad, 1, axis=0)
    back_upper = jnp.roll(lower_grad, -1, axis=0)
    returned = jnp.concatenate([back_lower, back_upper], 2).reshape(device_count, 2 * HALO_CAP, feat_dim)
    halo_part = jax.vmap(lambda values_in, indices: jax.ops.segment_sum(values_in, indices, NODE_DEV))(returned, cut_lists.reshape(device_count, 2 * HALO_CAP))
    node_total = node_local + part_grad.reshape(device_count, NODE_DEV, feat_dim) + halo_part
    node_grad = node_total.astype(jnp.bfloat16)
    pool_grad = jax.vmap(lambda values_in, indices: jnp.zeros((NODE_DEV + N_DOM * RELAY_CAP, feat_dim), jnp.bfloat16).at[indices].set(values_in))(node_grad, places.reshape(device_count, NODE_DEV))
    stay_grad = pool_grad[:, :NODE_DEV]
    slot_grad = pool_grad[:, NODE_DEV:].reshape(N_DOM, N_TILE, N_DOM, RELAY_CAP, feat_dim)
    sent_grad = jnp.transpose(slot_grad, (2, 1, 0, 3, 4)).reshape(device_count, N_DOM * RELAY_CAP, feat_dim)
    tile_grad = jax.vmap(lambda base_rows, values_in, indices: base_rows.at[indices].add(values_in))(stay_grad, sent_grad, pick_list.reshape(device_count, N_DOM * RELAY_CAP))
    return (node_new.reshape(NODES, feat_dim), edge_new.reshape(EDGES, feat_dim), tile_grad.reshape(NODES, feat_dim), edge_grad.reshape(EDGES, feat_dim), grad_total)
```

```python
import functools

import jax
import jax.numpy as jnp
from jax import lax
from jax.experimental import pallas as pl
from jax.experimental.pallas import tpu as pltpu
from jax.sharding import PartitionSpec as P

EPSILON = 1e-05
BF16 = jnp.bfloat16
F32 = jnp.float32
ROWS = 256
CHUNK = 32
VMEM_LIMIT = 30 * 1024 * 1024
SMALL_LIMIT = 8 * 1024 * 1024


def layer_norm(values):
    center = values - jnp.mean(values, -1, keepdims=True)
    inverse = lax.rsqrt(jnp.mean(center * center, -1, keepdims=True) + EPSILON)
    return (center * inverse, inverse)


def norm_grad(normed, inverse, upstream):
    mean_up = jnp.mean(upstream, -1, keepdims=True)
    mean_cross = jnp.mean(upstream * normed, -1, keepdims=True)
    return inverse * (upstream - mean_up - normed * mean_cross)


def silu_pair(values):
    sigmoid = 0.5 * jnp.tanh(0.5 * values) + 0.5
    return values * sigmoid, sigmoid * (1.0 + values * (1.0 - sigmoid))


def flat_dot(left_mat, right_mat):
    return jnp.dot(left_mat, right_mat, preferred_element_type=F32)


def inner_dot(left_mat, right_mat):
    return lax.dot_general(
        left_mat, right_mat, (((0,), (0,)), ((), ())), preferred_element_type=F32
    )


def outer_dot(left_mat, right_mat):
    return lax.dot_general(
        left_mat, right_mat, (((1,), (1,)), ((), ())), preferred_element_type=F32
    )


def split_parts(values):
    high_part = values.astype(BF16)
    return high_part, (values - high_part.astype(F32)).astype(BF16)


def marks(hits):
    return jnp.where(hits, 1.0, 0.0).astype(BF16)


def hot_columns(index_row, count, first=0):
    shape = (count, index_row.shape[-1])
    at = lax.broadcasted_iota(jnp.int32, shape, 0) + first
    return marks(jnp.broadcast_to(index_row.reshape(1, -1), shape) == at)


def as_column(index_row):
    shape = (128, index_row.shape[-1])
    return jnp.transpose(jnp.broadcast_to(index_row.reshape(1, -1), shape))


def hot_rows(index_column, count):
    at = lax.broadcasted_iota(jnp.int32, index_column.shape, 1)
    return jnp.concatenate(
        [marks(index_column == at + 128 * k) for k in range(count // 128)], 1
    )


class Kept:
    def __init__(self, array):
        self.array = array


def call(kernel, name, outs, ins, scratch, scalars=(), limit=VMEM_LIMIT):
    def spec(array):
        return pl.BlockSpec(memory_space=pltpu.VMEM if isinstance(array, Kept) else pltpu.HBM)

    def placed(array):
        if isinstance(array, Kept):
            return array.array
        return pltpu.with_memory_space_constraint(array, pltpu.HBM)

    shapes = [
        pltpu.SemaphoreType.DMA((s,)) if isinstance(s, int) else pltpu.VMEM(s.shape, s.dtype)
        for s in scratch
    ]
    return pl.pallas_call(
        kernel,
        out_shape=[
            array.array if isinstance(array, Kept) else pltpu.HBM(array.shape, array.dtype)
            for array in outs
        ],
        in_specs=[pl.BlockSpec(memory_space=pltpu.SMEM)] * len(scalars) + [spec(a) for a in ins],
        out_specs=[spec(array) for array in outs],
        scratch_shapes=shapes,
        compiler_params=pltpu.CompilerParams(vmem_limit_bytes=limit),
        name=name,
    )(*scalars, *[placed(array) for array in ins])


class Copies:
    def __init__(self, sems):
        self.sems = sems
        self.made = 0
        self.open = []

    def start(self, source, target):
        copy = pltpu.make_async_copy(source, target, self.sems.at[self.made])
        copy.start()
        self.made += 1
        self.open.append(copy)
        return copy

    def finish(self):
        for copy in self.open:
            copy.wait()


def pick_kernel(pick_hbm, tile_hbm, out_ref, pick_ref, pick, tile, in_sems):
    loads = Copies(in_sems)
    loads.start(pick_hbm, pick)
    loads.start(tile_hbm, tile)
    loads.finish()
    pick_ref[...] = pick[...]
    rows = hot_rows(as_column(pick[...]), tile.shape[0])
    out_ref[...] = flat_dot(rows, tile[...]).astype(BF16)


def pool_kernel(
    where_ref,
    from_hbm,
    cut_hbm,
    tile_hbm,
    came_ref,
    latent_ref,
    first_ref,
    second_ref,
    from_ref,
    cut_ref,
    at,
    cut,
    tile,
    ends,
    in_sems,
):
    loads = Copies(in_sems)
    for source, target in ((from_hbm, at), (cut_hbm, cut), (tile_hbm, tile)):
        loads.start(source, target)
    loads.finish()
    from_ref[...] = at[...].reshape(from_ref.shape)
    cut_ref[...] = cut[...]
    nodes = tile.shape[0]
    halo = first_ref.shape[0]
    rows = hot_rows(as_column(at[...]), nodes + came_ref.shape[0])
    value = flat_dot(rows[:, :nodes], tile[...]) + flat_dot(rows[:, nodes:], came_ref[...])
    value = value.astype(BF16)
    latent_ref[...] = value
    ends[...] = inner_dot(hot_columns(cut[...], nodes), value).astype(BF16)
    turn = pl.multiple_of(where_ref[2], halo)
    first_ref[...] = ends[pl.ds(turn, halo), :]
    second_ref[...] = ends[pl.ds(halo - turn, halo), :]


def base_kernel(
    receiver_hbm,
    edge_hbm,
    edge_in_hbm,
    edge_out_hbm,
    latent_ref,
    base_ref,
    w_send_ref,
    edge_out_ref,
    receiver,
    edge_lat,
    w_edge,
    w_recv,
    in_sems,
):
    feat = edge_out_ref.shape[0]
    loads = Copies(in_sems)
    first = [
        loads.start(receiver_hbm, receiver),
        loads.start(edge_hbm, edge_lat),
        loads.start(edge_in_hbm.at[0:feat], w_edge),
        loads.start(edge_in_hbm.at[2 * feat : 3 * feat], w_recv),
    ]
    second = [
        loads.start(edge_in_hbm.at[feat : 2 * feat], w_send_ref),
        loads.start(edge_out_hbm, edge_out_ref),
    ]
    for copy in first:
        copy.wait()
    column = as_column(receiver[...])
    latent = latent_ref[...]
    for at in range(0, edge_lat.shape[0], ROWS):
        rows = slice(at, at + ROWS)
        taken = flat_dot(hot_rows(column[rows], latent.shape[0]), latent).astype(BF16)
        base_ref[rows, :] = flat_dot(edge_lat[rows, :], w_edge[...]) + flat_dot(taken, w_recv[...])
    for copy in second:
        copy.wait()


def put(weights, first, terms):
    for t in range(terms.shape[1] // 128):
        weights[t, first : first + terms.shape[0], :] = terms[:, t * 128 : (t + 1) * 128].astype(
            BF16
        )


def block_kernel(
    places,
    where_ref,
    sender_hbm,
    receiver_hbm,
    latent_ref,
    near_ref,
    far_ref,
    cross_ref,
    first_ref,
    second_ref,
    base_ref,
    w_send,
    edge_out,
    edge_hbm,
    edge_t_hbm,
    w_recv_hbm,
    node_in_hbm,
    node_out_hbm,
    node_cot_hbm,
    edge_cot_hbm,
    node_new_hbm,
    edge_new_hbm,
    pre_grad_hbm,
    agg_parts_hbm,
    local_ref,
    keep_upper_ref,
    keep_lower_ref,
    send_upper_ref,
    send_lower_ref,
    own_ref,
    opposite_ref,
    back_first_ref,
    back_second_ref,
    sender,
    receiver,
    table,
    edge_lat,
    edge_t,
    picked,
    w_recv,
    node_x,
    node_in,
    node_out,
    node_cot,
    edge_cot,
    node_new,
    node_act,
    node_lin_grad,
    node_pre_grad,
    agg_parts,
    node_work,
    node_slope,
    edge_new,
    act,
    lin_grad,
    pre_grad,
    work,
    slope,
    normed,
    inverse,
    edge_up,
    back_work,
    weights,
    sums,
    core_sums,
    in_sems,
    out_sems,
):
    feat = edge_out.shape[0]
    nodes = node_cot.shape[0]
    edges = edge_lat.shape[0]
    halo = first_ref.shape[0]
    tiles, _, width = weights.shape
    core = where_ref[0]
    tile = where_ref[1]
    turn = pl.multiple_of(where_ref[2], halo)
    part = tiles * nodes
    held = part + 2 * halo
    loads = Copies(in_sems)
    stores = Copies(out_sems)

    def rows_of(mask):
        return pl.ds(pl.multiple_of((tile ^ mask) * nodes, nodes), nodes)

    first = [
        loads.start(sender_hbm, sender),
        loads.start(receiver_hbm, receiver),
    ]
    second = [loads.start(edge_hbm, edge_lat)]
    third = [
        loads.start(node_in_hbm, node_in),
        loads.start(node_out_hbm, node_out),
        loads.start(node_cot_hbm, node_cot),
    ]
    fourth = [loads.start(edge_cot_hbm, edge_cot)]
    fifth = [
        loads.start(edge_t_hbm, edge_t),
        loads.start(w_recv_hbm.at[2 * feat : 3 * feat], w_recv),
    ]

    for mask, ref in enumerate((latent_ref, near_ref, far_ref, cross_ref)):
        table[rows_of(mask), :] = ref[...]
    table[pl.ds(part + turn, halo), :] = first_ref[...]
    table[pl.ds(part + halo - turn, halo), :] = second_ref[...]
    table[held:, :] = jnp.zeros((table.shape[0] - held, feat), BF16)
    for copy in first:
        copy.wait()
    latent = latent_ref[...]
    node_x[:, 0:feat] = latent
    sender_column = as_column(sender[...])
    receiver_hot = hot_rows(as_column(receiver[...]), nodes)
    receiver_rows = hot_columns(receiver[...], nodes)
    blocks = [slice(at, at + ROWS) for at in range(0, edges, ROWS)]

    def chunks(rows):
        return [slice(at, at + CHUNK) for at in range(rows.start, rows.stop, CHUNK)]

    for rows in blocks:
        hot = hot_rows(sender_column[rows], table.shape[0])
        picked[rows, :] = flat_dot(hot, table[...]).astype(BF16)
    for rows in blocks:
        work[rows, :] = flat_dot(picked[rows, :], w_send[...])
        for c in chunks(rows):
            value, slope[c, :] = silu_pair(base_ref[c, :] + work[c, :])
            act[c, :] = value.astype(BF16)
        normed[rows, :] = flat_dot(act[rows, :], edge_out[...])
        if rows.start == 0:
            for copy in second:
                copy.wait()
        for c in chunks(rows):
            value, scale = layer_norm(normed[c, :])
            normed[c, :] = value
            inverse[c, :] = scale
            edge_new[c, :] = (edge_lat[c, :].astype(F32) + value).astype(BF16)
    stores.start(edge_new, edge_new_hbm)
    node_x[:, feat:] = flat_dot(receiver_rows, edge_new[...]).astype(BF16)

    for copy in third:
        copy.wait()
    node_rows = slice(0, nodes)
    node_work[...] = flat_dot(node_x[...], node_in[...])
    for c in chunks(node_rows):
        value, node_slope[c, :] = silu_pair(node_work[c, :])
        node_act[c, :] = value.astype(BF16)
    node_work[...] = flat_dot(node_act[...], node_out[...])
    for c in chunks(node_rows):
        value, scale = layer_norm(node_work[c, :])
        node_new[c, :] = (node_x[c, 0:feat].astype(F32) + value).astype(BF16)
        up = node_cot[c, :].astype(F32)
        node_lin_grad[c, :] = norm_grad(value, scale, up).astype(BF16)
    stores.start(node_new, node_new_hbm)
    node_work[...] = outer_dot(node_lin_grad[...], node_out[...])
    for c in chunks(node_rows):
        node_pre_grad[c, :] = (node_work[c, :] * node_slope[c, :]).astype(BF16)
    node_work[...] = outer_dot(node_pre_grad[...], node_in[feat:, :])
    for c in chunks(node_rows):
        agg_parts[c, :], low_part = split_parts(node_work[c, :])
        agg_parts[slice(c.start + nodes, c.stop + nodes), :] = low_part
    stores.start(agg_parts, agg_parts_hbm)

    for copy in fourth:
        copy.wait()
    for rows in blocks:
        hot = receiver_hot[rows]
        edge_up[rows, :] = flat_dot(jnp.concatenate([hot, hot], 1), agg_parts[...])
        for c in chunks(rows):
            up = edge_cot[c, :].astype(F32) + edge_up[c, :]
            edge_up[c, :] = up
            lin_grad[c, :] = norm_grad(normed[c, :], inverse[c, :], up).astype(BF16)
        back_work[rows, :] = outer_dot(lin_grad[rows, :], edge_out[...])
        for c in chunks(rows):
            pre_grad[c, :] = (back_work[c, :] * slope[c, :]).astype(BF16)
    stores.start(pre_grad, pre_grad_hbm)
    taken = flat_dot(receiver_rows, pre_grad[...])

    def give(which, keep_ref, send_ref):
        for source, rows, first, count in places[which]:
            to = pl.ds(first, count)
            stores.start(weights.at[2 * source + core, rows], keep_ref.at[to])
            stores.start(weights.at[2 * source + 1 - core, rows], send_ref.at[to])

    part_rows = sums.shape[0] // 2
    for start in (0, part_rows):
        sums[start : start + part_rows, :] = flat_dot(
            hot_columns(sender[...], part_rows, start), pre_grad[...]
        )
    back_first_ref[...] = sums[pl.ds(part + turn, halo), :].astype(BF16)
    back_second_ref[...] = sums[pl.ds(part + halo - turn, halo), :].astype(BF16)
    for mask, ref, first in (
        (0, own_ref, 0),
        (2, opposite_ref, 0),
        (1, core_sums, 0),
        (3, core_sums, part),
    ):
        value = sums[rows_of(mask), :].astype(ref.dtype)
        for at in range(tiles):
            lanes = slice(at * width, (at + 1) * width)
            ref[first + at * nodes : first + (at + 1) * nodes, :] = value[:, lanes]
    stores.start(core_sums, send_upper_ref.at[pl.ds(send_lower_ref.shape[0], 2 * part)])
    put(weights, 4 * feat, inner_dot(node_x[...], node_pre_grad[...]))
    put(weights, 6 * feat, inner_dot(node_act[...], node_lin_grad[...]))
    put(weights, 3 * feat, inner_dot(act[...], lin_grad[...]))
    give(0, keep_upper_ref, send_upper_ref)
    high_part, low_part = split_parts(taken)
    put(weights, 2 * feat, inner_dot(latent, high_part) + inner_dot(latent, low_part))
    put(weights, feat, inner_dot(picked[...], pre_grad[...]))
    for copy in fifth:
        copy.wait()
    put(weights, 0, flat_dot(edge_t[...], pre_grad[...]))
    give(1, keep_lower_ref, send_lower_ref)
    local_ref[...] = (
        node_cot[...].astype(F32)
        + outer_dot(node_pre_grad[...], node_in[0:feat, :])
        + (outer_dot(high_part, w_recv[...]) + outer_dot(low_part, w_recv[...]))
    )
    stores.finish()


def edge_grad_kernel(
    receiver_hbm,
    pre_grad_hbm,
    edge_cot_hbm,
    w_hbm,
    agg_parts_hbm,
    out_hbm,
    receiver,
    pre_grad,
    edge_cot,
    w_edge,
    agg_parts,
    work,
    out,
    in_sems,
    out_sems,
):
    loads, stores = Copies(in_sems), Copies(out_sems)
    for source, target in (
        (receiver_hbm, receiver),
        (agg_parts_hbm, agg_parts),
        (w_hbm.at[0 : w_edge.shape[0]], w_edge),
        (pre_grad_hbm, pre_grad),
        (edge_cot_hbm, edge_cot),
    ):
        loads.start(source, target)
    loads.finish()
    column = as_column(receiver[...])
    for at in range(0, out.shape[0], ROWS):
        rows = slice(at, at + ROWS)
        hot = hot_rows(column[rows], agg_parts.shape[0] // 2)
        work[rows, :] = flat_dot(jnp.concatenate([hot, hot], 1), agg_parts[...]) + outer_dot(
            pre_grad[rows, :], w_edge[...]
        )
        for start in range(at, at + ROWS, CHUNK):
            c = slice(start, start + CHUNK)
            out[c, :] = (edge_cot[c, :].astype(F32) + work[c, :]).astype(BF16)
        stores.start(out.at[rows], out_hbm.at[rows])
    stores.finish()


def node_kernel(
    where_ref,
    from_ref,
    cut_ref,
    w_send_ref,
    local_ref,
    total_ref,
    first_ref,
    second_ref,
    stay_ref,
    slot_ref,
    ends,
):
    nodes, feat = local_ref.shape
    halo = first_ref.shape[0]
    width = total_ref.shape[1]
    turn = pl.multiple_of(where_ref[2], halo)
    ends[pl.ds(turn, halo), :] = first_ref[...]
    ends[pl.ds(halo - turn, halo), :] = second_ref[...]
    value = jnp.concatenate(
        [total_ref[block * nodes : (block + 1) * nodes, :] for block in range(feat // width)], 1
    )
    value = value + flat_dot(hot_columns(cut_ref[...], nodes), ends[...])
    high_part, low_part = split_parts(value)
    w_send = w_send_ref[...]
    grad = local_ref[...] + (outer_dot(high_part, w_send) + outer_dot(low_part, w_send))
    grad = grad.astype(BF16)
    where = from_ref[...]
    slot_ref[...] = flat_dot(hot_columns(where, slot_ref.shape[0], nodes), grad).astype(BF16)
    stay_ref[...] = flat_dot(hot_columns(where, nodes), grad).astype(BF16)


def back_kernel(pick_ref, stay_ref, came_ref, out_hbm, out, out_sems):
    stores = Copies(out_sems)
    hot = hot_columns(pick_ref[...], stay_ref.shape[0])
    out[...] = (stay_ref[...].astype(F32) + flat_dot(hot, came_ref[...])).astype(BF16)
    stores.start(out, out_hbm)
    stores.finish()


def flip(values, axis, mask):
    count = lax.axis_size(axis)
    return lax.ppermute(values, axis, [(i, i ^ mask) for i in range(count)])


def meet(values, axis, step):
    count = lax.axis_size(axis)
    pairs = [(i, (i + (step if i % 2 == 0 else -step)) % count) for i in range(count)]
    return lax.ppermute(values, axis, pairs)


def axis_bits(axis):
    return [(axis, b) for b in range(lax.axis_size(axis).bit_length() - 1)]


def exchange_orders():
    cross, dom_bits = axis_bits("tile")[1:], axis_bits("dom")
    side, line = dom_bits[:1], dom_bits[1:-1]
    return side + cross + line, line + side + cross


def block_places(order, rows, low):
    found = []
    for index in range(1 << len(order)):
        upper = block = 0
        for at, (axis, bit) in enumerate(order):
            value = (index >> (len(order) - 1 - at)) & 1
            if axis == "tile":
                upper |= value << (bit - 1)
            else:
                block |= value << bit
        start = low + block * rows
        found.append((upper, slice(start, start + rows), index * rows, rows))
    return found


def after(values, *others):
    return lax.optimization_barrier((values, others))[0]


def total_of(values):
    return functools.reduce(jnp.add, [v.astype(F32) for v in values])


class Exchange:
    def __init__(self, values, count, order):
        self.values = values
        self.count = count
        self.order = list(order)
        self.outgoing = None

    def rows(self, arrays, skip):
        found = [
            lax.dynamic_slice_in_dim(array, row + skip, self.count, 0)
            for array, (_, row) in zip(arrays, self.values)
        ]
        return total_of(found)

    def cut(self, *others):
        arrays = after([array for array, _ in self.values], *others)
        self.count //= 2
        axis, bit = self.order[0]
        mine = (lax.axis_index(axis) >> bit) & 1
        self.outgoing = self.rows(arrays, (1 - mine) * self.count).astype(BF16)
        self.values = [(self.rows(arrays, mine * self.count).astype(BF16), 0)]
        return self.outgoing

    def send(self):
        axis, bit = self.order.pop(0)
        self.values.append((flip(self.outgoing, axis, 1 << bit), 0))

    def total(self):
        return self.rows([array for array, _ in self.values], 0)


def cut_all(parts, *others):
    return [part.cut(*others) for part in parts]


def send_all(parts):
    for part in parts:
        part.send()


def body(
    tile_latent,
    relay_pick,
    relay_from,
    cut_pick,
    edge_latent,
    edge_sender,
    edge_receiver,
    edge_in,
    edge_out,
    node_in,
    node_out,
    node_cot,
    edge_cot,
):
    nodes, feat = tile_latent.shape
    edges = edge_latent.shape[0]
    doms, tiles = lax.axis_size("dom"), lax.axis_size("tile")
    slots = relay_pick.shape[1]
    halo = cut_pick.shape[1] // 2
    table_rows = -(-(tiles * nodes + 2 * halo) // nodes) * nodes
    half, width = 7 * feat // 2, feat // tiles
    sds = jax.ShapeDtypeStruct
    node_bf16 = sds((nodes, feat), BF16)
    node_f32 = sds((nodes, feat), F32)
    edge_bf16 = sds((edges, feat), BF16)
    edge_f32 = sds((edges, feat), F32)
    slot_bf16 = sds((slots, feat), BF16)
    halo_bf16 = sds((halo, feat), BF16)
    square = sds((feat, feat), BF16)
    node_index = sds((nodes,), jnp.int32)
    edge_index = sds((edges,), jnp.int32)

    def exchange(rows):
        blocks = rows.reshape(doms, slots // doms, feat)
        return lax.all_to_all(blocks, "dom", split_axis=0, concat_axis=0, tiled=True).reshape(
            slots, feat
        )

    tile = lax.axis_index("tile")
    turn = jnp.where(lax.axis_index("dom") % 2 == 0, halo, 0)
    where = jnp.stack([tile & 1, tile, turn]).astype(jnp.int32)
    outgoing, pick_row = call(
        pick_kernel,
        "pick",
        [Kept(slot_bf16), Kept(relay_pick)],
        [relay_pick, tile_latent],
        [relay_pick, tile_latent, 2],
        limit=SMALL_LIMIT,
    )
    edge_t = jnp.transpose(after(edge_latent, outgoing))
    came = after(exchange(outgoing), edge_t)
    latent, first, second, from_row, cut_row = call(
        pool_kernel,
        "pool",
        [Kept(node_bf16), Kept(halo_bf16), Kept(halo_bf16)]
        + [Kept(sds((1, nodes), jnp.int32)), Kept(cut_pick)],
        [relay_from, cut_pick, tile_latent, Kept(came)],
        [node_index, cut_pick, node_bf16, sds((2 * halo, feat), BF16), 3],
        [where],
        SMALL_LIMIT,
    )
    far = flip(latent, "tile", 2)
    near = flip(latent, "tile", 1)
    first = meet(first, "dom", 1)
    second = meet(second, "dom", -1)
    base, w_send, w_out = call(
        base_kernel,
        "base",
        [Kept(edge_f32), Kept(square), Kept(square)],
        [edge_receiver, edge_latent, edge_in, edge_out, Kept(latent)],
        [edge_index, edge_bf16, square, square, 6],
    )
    across = flip(after(far, first, second, base), "tile", 1)

    orders = exchange_orders()
    rows = 7 * feat // doms
    bits = len(orders[0])
    fine = rows % 16 == 0
    span = tiles * half // 2
    if fine:
        places = [block_places(order, rows, low) for order, low in zip(orders, (half, 0))]
    else:
        places = [
            [(at, slice(low, low + half), at * half, half) for at in range(tiles // 2)]
            for low in (half, 0)
        ]
    sum_rows = tiles * nodes
    (
        node_new,
        edge_new,
        pre_grad,
        agg_parts,
        local,
        keep_upper,
        keep_lower,
        send_upper,
        send_lower,
        own,
        opposite,
        back_first,
        back_second,
    ) = call(
        functools.partial(block_kernel, places),
        "block",
        [node_bf16, edge_bf16, edge_bf16, sds((2 * nodes, feat), BF16), Kept(node_f32)]
        + [sds((span, width), BF16)] * 2
        + [sds((span + 2 * sum_rows, width), BF16), sds((span, width), BF16)]
        + [Kept(sds((sum_rows, width), F32)), Kept(sds((sum_rows, width), BF16))]
        + [Kept(halo_bf16)] * 2,
        [edge_sender, edge_receiver]
        + [Kept(array) for array in (latent, near, far, across, first, second)]
        + [Kept(base), Kept(w_send), Kept(w_out)]
        + [edge_latent, edge_t, edge_in, node_in, node_out, node_cot, edge_cot],
        [edge_index, edge_index, sds((table_rows, feat), BF16), edge_bf16]
        + [sds((feat, edges), BF16), edge_bf16, square, sds((nodes, 2 * feat), BF16)]
        + [node_in, node_out, node_cot, edge_cot]
        + [node_bf16] * 4
        + [sds((2 * nodes, feat), BF16), node_f32, node_f32]
        + [edge_bf16] * 4
        + [edge_f32] * 3
        + [sds((edges, 1), F32), edge_f32, edge_f32]
        + [sds((tiles, 2 * half, width), BF16), sds((table_rows, feat), F32)]
        + [sds((2 * sum_rows, width), BF16)]
        + [9, 5 + 2 * sum(len(place) for place in places)],
        [where],
    )
    got_upper = flip(send_upper, "tile", 1)
    got_lower = flip(send_lower, "tile", 1)
    back_first = meet(back_first, "dom", 1)
    back_second = meet(back_second, "dom", -1)
    across = opposite.astype(F32) + got_upper[span + sum_rows :].astype(F32)
    across = flip(across.astype(BF16), "tile", 2)
    parts = []
    for order, keep, got in zip(
        orders, (keep_upper, keep_lower), (got_upper, got_lower), strict=True
    ):
        if fine:
            parts.append(Exchange([(keep, 0), (got, 0)], span, order))
            continue
        labels = axis_bits("tile")[:0:-1] + axis_bits("dom")[-2::-1]
        axes = [labels.index(label) for label in order] + [bits, bits + 1]
        values = [
            jnp.transpose(whole.reshape([2] * bits + [rows, width]), axes)
            for whole in (keep, got[:span])
        ]
        parts.append(Exchange([(v.reshape(span, width), 0) for v in values], span, order))
    sent = parts[0].cut()
    parts[0].send()
    sent = parts[1].cut(sent, back_first, back_second)
    parts[1].send()
    total = own + got_upper[span : span + sum_rows].astype(F32) + across.astype(F32)
    stay, slot_grad = call(
        node_kernel,
        "node",
        [Kept(node_bf16), Kept(slot_bf16)],
        [Kept(array) for array in (from_row, cut_row, w_send, after(local, sent), total)]
        + [Kept(back_first), Kept(back_second)],
        [sds((2 * halo, feat), BF16)],
        [where],
        SMALL_LIMIT,
    )
    back_rows = exchange(slot_grad)
    sent = cut_all(parts, slot_grad)
    send_all(parts)
    [latent_grad] = call(
        back_kernel,
        "back",
        [node_bf16],
        [Kept(pick_row), Kept(stay), Kept(after(back_rows, *sent))],
        [node_bf16, 1],
        limit=SMALL_LIMIT,
    )
    [edge_grad] = call(
        edge_grad_kernel,
        "edge_grad",
        [edge_bf16],
        [edge_receiver, after(pre_grad, latent_grad), edge_cot, edge_in, agg_parts],
        [edge_index, edge_bf16, edge_bf16, square, sds((2 * nodes, feat), BF16)]
        + [edge_f32, edge_bf16, 5, edges // ROWS],
        limit=2 * SMALL_LIMIT,
    )
    first = edge_grad
    while parts[0].order:
        cut_all(parts, first)
        send_all(parts)
        first = ()
    top = axis_bits("dom")[-1][1]
    upper = (lax.axis_index("dom") >> top) & 1
    above, below = [part.total() for part in parts]
    sent = jnp.where(upper == 1, below, above).astype(BF16)
    kept = jnp.where(upper == 1, above, below)
    weight_shard = kept + flip(sent, "dom", 1 << top).astype(F32)
    return (node_new, edge_new, latent_grad, edge_grad, weight_shard)


def solution(mesh):
    rows = P(("dom", "tile"), None)
    flat = P(("dom", "tile"))
    in_specs = (rows, rows, flat, rows, rows, flat, flat, P(), P(), P(), P(), rows, rows)
    out_specs = (rows, rows, rows, rows, P("dom", "tile"))
    return jax.shard_map(body, mesh=mesh, in_specs=in_specs, out_specs=out_specs, check_vma=False)
```

```python
import functools

import jax
import jax.numpy as jnp
from jax import lax
from jax.experimental import pallas as pl
from jax.experimental.pallas import tpu as pltpu
from jax.sharding import PartitionSpec as P

EPSILON = 1e-05
BF16 = jnp.bfloat16
F32 = jnp.float32
ROWS = 256
CHUNK = 32
VMEM_LIMIT = 30 * 1024 * 1024
SMALL_LIMIT = 8 * 1024 * 1024


def layer_norm(values):
    center = values - jnp.mean(values, -1, keepdims=True)
    inverse = lax.rsqrt(jnp.mean(center * center, -1, keepdims=True) + EPSILON)
    return (center * inverse, inverse)


def norm_grad(normed, inverse, upstream):
    mean_up = jnp.mean(upstream, -1, keepdims=True)
    mean_cross = jnp.mean(upstream * normed, -1, keepdims=True)
    return inverse * (upstream - mean_up - normed * mean_cross)


def silu_pair(values):
    sigmoid = 0.5 * jnp.tanh(0.5 * values) + 0.5
    return values * sigmoid, sigmoid * (1.0 + values * (1.0 - sigmoid))


def flat_dot(left_mat, right_mat):
    return jnp.dot(left_mat, right_mat, preferred_element_type=F32)


def inner_dot(left_mat, right_mat):
    return lax.dot_general(
        left_mat, right_mat, (((0,), (0,)), ((), ())), preferred_element_type=F32
    )


def outer_dot(left_mat, right_mat):
    return lax.dot_general(
        left_mat, right_mat, (((1,), (1,)), ((), ())), preferred_element_type=F32
    )


def split_parts(values):
    high_part = values.astype(BF16)
    return high_part, (values - high_part.astype(F32)).astype(BF16)


def marks(hits):
    return jnp.where(hits, 1.0, 0.0).astype(BF16)


def hot_columns(index_row, count, first=0):
    shape = (count, index_row.shape[-1])
    at = lax.broadcasted_iota(jnp.int32, shape, 0) + first
    return marks(jnp.broadcast_to(index_row.reshape(1, -1), shape) == at)


def as_column(index_row):
    shape = (128, index_row.shape[-1])
    return jnp.transpose(jnp.broadcast_to(index_row.reshape(1, -1), shape))


def hot_rows(index_column, count):
    at = lax.broadcasted_iota(jnp.int32, index_column.shape, 1)
    return jnp.concatenate(
        [marks(index_column == at + 128 * k) for k in range(count // 128)], 1
    )


class Kept:
    def __init__(self, array):
        self.array = array


def call(kernel, name, outs, ins, scratch, scalars=(), limit=VMEM_LIMIT):
    def spec(array):
        return pl.BlockSpec(memory_space=pltpu.VMEM if isinstance(array, Kept) else pltpu.HBM)

    def placed(array):
        if isinstance(array, Kept):
            return array.array
        return pltpu.with_memory_space_constraint(array, pltpu.HBM)

    shapes = [
        pltpu.SemaphoreType.DMA((s,)) if isinstance(s, int) else pltpu.VMEM(s.shape, s.dtype)
        for s in scratch
    ]
    return pl.pallas_call(
        kernel,
        out_shape=[
            array.array if isinstance(array, Kept) else pltpu.HBM(array.shape, array.dtype)
            for array in outs
        ],
        in_specs=[pl.BlockSpec(memory_space=pltpu.SMEM)] * len(scalars) + [spec(a) for a in ins],
        out_specs=[spec(array) for array in outs],
        scratch_shapes=shapes,
        compiler_params=pltpu.CompilerParams(vmem_limit_bytes=limit),
        name=name,
    )(*scalars, *[placed(array) for array in ins])


class Copies:
    def __init__(self, sems):
        self.sems = sems
        self.made = 0
        self.open = []

    def start(self, source, target):
        copy = pltpu.make_async_copy(source, target, self.sems.at[self.made])
        copy.start()
        self.made += 1
        self.open.append(copy)
        return copy

    def finish(self):
        for copy in self.open:
            copy.wait()


def pick_kernel(pick_hbm, tile_hbm, out_ref, pick_ref, pick, tile, in_sems):
    loads = Copies(in_sems)
    loads.start(pick_hbm, pick)
    loads.start(tile_hbm, tile)
    loads.finish()
    pick_ref[...] = pick[...]
    rows = hot_rows(as_column(pick[...]), tile.shape[0])
    out_ref[...] = flat_dot(rows, tile[...]).astype(BF16)


def pool_kernel(
    where_ref,
    from_hbm,
    cut_hbm,
    tile_hbm,
    came_ref,
    latent_ref,
    first_ref,
    second_ref,
    from_ref,
    cut_ref,
    at,
    cut,
    tile,
    ends,
    in_sems,
):
    loads = Copies(in_sems)
    for source, target in ((from_hbm, at), (cut_hbm, cut), (tile_hbm, tile)):
        loads.start(source, target)
    loads.finish()
    from_ref[...] = at[...].reshape(from_ref.shape)
    cut_ref[...] = cut[...]
    nodes = tile.shape[0]
    halo = first_ref.shape[0]
    rows = hot_rows(as_column(at[...]), nodes + came_ref.shape[0])
    value = flat_dot(rows[:, :nodes], tile[...]) + flat_dot(rows[:, nodes:], came_ref[...])
    value = value.astype(BF16)
    latent_ref[...] = value
    ends[...] = inner_dot(hot_columns(cut[...], nodes), value).astype(BF16)
    turn = pl.multiple_of(where_ref[2], halo)
    first_ref[...] = ends[pl.ds(turn, halo), :]
    second_ref[...] = ends[pl.ds(halo - turn, halo), :]


def base_kernel(
    receiver_hbm,
    edge_hbm,
    edge_in_hbm,
    edge_out_hbm,
    latent_ref,
    base_ref,
    w_send_ref,
    edge_out_ref,
    receiver,
    edge_lat,
    w_edge,
    w_recv,
    in_sems,
):
    feat = edge_out_ref.shape[0]
    loads = Copies(in_sems)
    first = [
        loads.start(receiver_hbm, receiver),
        loads.start(edge_hbm, edge_lat),
        loads.start(edge_in_hbm.at[0:feat], w_edge),
        loads.start(edge_in_hbm.at[2 * feat : 3 * feat], w_recv),
    ]
    second = [
        loads.start(edge_in_hbm.at[feat : 2 * feat], w_send_ref),
        loads.start(edge_out_hbm, edge_out_ref),
    ]
    for copy in first:
        copy.wait()
    column = as_column(receiver[...])
    latent = latent_ref[...]
    for at in range(0, edge_lat.shape[0], ROWS):
        rows = slice(at, at + ROWS)
        taken = flat_dot(hot_rows(column[rows], latent.shape[0]), latent).astype(BF16)
        base_ref[rows, :] = flat_dot(edge_lat[rows, :], w_edge[...]) + flat_dot(taken, w_recv[...])
    for copy in second:
        copy.wait()


def put(weights, first, terms):
    for t in range(terms.shape[1] // 128):
        weights[t, first : first + terms.shape[0], :] = terms[:, t * 128 : (t + 1) * 128].astype(
            BF16
        )


def block_kernel(
    places,
    where_ref,
    sender_hbm,
    receiver_hbm,
    latent_ref,
    near_ref,
    far_ref,
    cross_ref,
    first_ref,
    second_ref,
    base_ref,
    w_send,
    edge_out,
    edge_hbm,
    edge_t_hbm,
    w_recv_hbm,
    node_in_hbm,
    node_out_hbm,
    node_cot_hbm,
    edge_cot_hbm,
    node_new_hbm,
    edge_new_hbm,
    pre_grad_hbm,
    agg_parts_hbm,
    local_ref,
    keep_upper_ref,
    keep_lower_ref,
    send_upper_ref,
    send_lower_ref,
    own_ref,
    opposite_ref,
    back_first_ref,
    back_second_ref,
    sender,
    receiver,
    table,
    edge_lat,
    edge_t,
    picked,
    w_recv,
    node_x,
    node_in,
    node_out,
    node_cot,
    edge_cot,
    node_new,
    node_act,
    node_lin_grad,
    node_pre_grad,
    agg_parts,
    node_work,
    node_slope,
    edge_new,
    act,
    lin_grad,
    pre_grad,
    work,
    slope,
    normed,
    inverse,
    edge_up,
    back_work,
    weights,
    sums,
    core_sums,
    in_sems,
    out_sems,
):
    feat = edge_out.shape[0]
    nodes = node_cot.shape[0]
    edges = edge_lat.shape[0]
    halo = first_ref.shape[0]
    tiles, _, width = weights.shape
    core = where_ref[0]
    tile = where_ref[1]
    turn = pl.multiple_of(where_ref[2], halo)
    part = tiles * nodes
    held = part + 2 * halo
    loads = Copies(in_sems)
    stores = Copies(out_sems)

    def rows_of(mask):
        return pl.ds(pl.multiple_of((tile ^ mask) * nodes, nodes), nodes)

    first = [
        loads.start(sender_hbm, sender),
        loads.start(receiver_hbm, receiver),
    ]
    second = [loads.start(edge_hbm, edge_lat)]
    third = [
        loads.start(node_in_hbm, node_in),
        loads.start(node_out_hbm, node_out),
        loads.start(node_cot_hbm, node_cot),
    ]
    fourth = [loads.start(edge_cot_hbm, edge_cot)]
    fifth = [
        loads.start(edge_t_hbm, edge_t),
        loads.start(w_recv_hbm.at[2 * feat : 3 * feat], w_recv),
    ]

    for mask, ref in enumerate((latent_ref, near_ref, far_ref, cross_ref)):
        table[rows_of(mask), :] = ref[...]
    table[pl.ds(part + turn, halo), :] = first_ref[...]
    table[pl.ds(part + halo - turn, halo), :] = second_ref[...]
    table[held:, :] = jnp.zeros((table.shape[0] - held, feat), BF16)
    for copy in first:
        copy.wait()
    latent = latent_ref[...]
    node_x[:, 0:feat] = latent
    sender_column = as_column(sender[...])
    receiver_hot = hot_rows(as_column(receiver[...]), nodes)
    receiver_rows = hot_columns(receiver[...], nodes)
    blocks = [slice(at, at + ROWS) for at in range(0, edges, ROWS)]

    def chunks(rows):
        return [slice(at, at + CHUNK) for at in range(rows.start, rows.stop, CHUNK)]

    for rows in blocks:
        hot = hot_rows(sender_column[rows], table.shape[0])
        picked[rows, :] = flat_dot(hot, table[...]).astype(BF16)
    for rows in blocks:
        work[rows, :] = flat_dot(picked[rows, :], w_send[...])
        for c in chunks(rows):
            value, slope[c, :] = silu_pair(base_ref[c, :] + work[c, :])
            act[c, :] = value.astype(BF16)
        normed[rows, :] = flat_dot(act[rows, :], edge_out[...])
        if rows.start == 0:
            for copy in second:
                copy.wait()
        for c in chunks(rows):
            value, scale = layer_norm(normed[c, :])
            normed[c, :] = value
            inverse[c, :] = scale
            edge_new[c, :] = (edge_lat[c, :].astype(F32) + value).astype(BF16)
    stores.start(edge_new, edge_new_hbm)
    node_x[:, feat:] = flat_dot(receiver_rows, edge_new[...]).astype(BF16)

    for copy in third:
        copy.wait()
    node_rows = slice(0, nodes)
    node_work[...] = flat_dot(node_x[...], node_in[...])
    for c in chunks(node_rows):
        value, node_slope[c, :] = silu_pair(node_work[c, :])
        node_act[c, :] = value.astype(BF16)
    node_work[...] = flat_dot(node_act[...], node_out[...])
    for c in chunks(node_rows):
        value, scale = layer_norm(node_work[c, :])
        node_new[c, :] = (node_x[c, 0:feat].astype(F32) + value).astype(BF16)
        up = node_cot[c, :].astype(F32)
        node_lin_grad[c, :] = norm_grad(value, scale, up).astype(BF16)
    stores.start(node_new, node_new_hbm)
    node_work[...] = outer_dot(node_lin_grad[...], node_out[...])
    for c in chunks(node_rows):
        node_pre_grad[c, :] = (node_work[c, :] * node_slope[c, :]).astype(BF16)
    node_work[...] = outer_dot(node_pre_grad[...], node_in[feat:, :])
    for c in chunks(node_rows):
        agg_parts[c, :], low_part = split_parts(node_work[c, :])
        agg_parts[slice(c.start + nodes, c.stop + nodes), :] = low_part
    stores.start(agg_parts, agg_parts_hbm)

    for copy in fourth:
        copy.wait()
    for rows in blocks:
        hot = receiver_hot[rows]
        edge_up[rows, :] = flat_dot(jnp.concatenate([hot, hot], 1), agg_parts[...])
        for c in chunks(rows):
            up = edge_cot[c, :].astype(F32) + edge_up[c, :]
            edge_up[c, :] = up
            lin_grad[c, :] = norm_grad(normed[c, :], inverse[c, :], up).astype(BF16)
        back_work[rows, :] = outer_dot(lin_grad[rows, :], edge_out[...])
        for c in chunks(rows):
            pre_grad[c, :] = (back_work[c, :] * slope[c, :]).astype(BF16)
    stores.start(pre_grad, pre_grad_hbm)
    taken = flat_dot(receiver_rows, pre_grad[...])

    def give(which, keep_ref, send_ref):
        order, low = places[which]
        half = keep_ref.shape[0] // (tiles // 2)
        if order is None:
            for upper in range(tiles // 2):
                to = pl.ds(upper * half, half)
                rows = slice(low, low + half)
                stores.start(weights.at[2 * upper + core, rows], keep_ref.at[to])
                stores.start(weights.at[2 * upper + 1 - core, rows], send_ref.at[to])
            return
        here = {"tile": tile, "dom": where_ref[3]}
        rows = keep_ref.shape[0] >> len(order)
        for index in range(1 << len(order)):
            upper = block = 0
            for at, (axis, bit) in enumerate(order):
                flipped = 1 - ((index >> (len(order) - 1 - at)) & 1)
                value = ((here[axis] >> bit) & 1) ^ flipped
                if axis == "tile":
                    upper = upper + (value << (bit - 1))
                else:
                    block = block + (value << bit)
            source = pl.ds(pl.multiple_of(low + block * rows, 16), rows)
            to = pl.ds(index * rows, rows)
            stores.start(weights.at[2 * upper + core, source], keep_ref.at[to])
            stores.start(weights.at[2 * upper + 1 - core, source], send_ref.at[to])

    part_rows = sums.shape[0] // 2
    for start in (0, part_rows):
        sums[start : start + part_rows, :] = flat_dot(
            hot_columns(sender[...], part_rows, start), pre_grad[...]
        )
    back_first_ref[...] = sums[pl.ds(part + turn, halo), :].astype(BF16)
    back_second_ref[...] = sums[pl.ds(part + halo - turn, halo), :].astype(BF16)
    for mask, ref, first in (
        (0, own_ref, 0),
        (2, opposite_ref, 0),
        (1, core_sums, 0),
        (3, core_sums, part),
    ):
        value = sums[rows_of(mask), :].astype(ref.dtype)
        for at in range(tiles):
            lanes = slice(at * width, (at + 1) * width)
            ref[first + at * nodes : first + (at + 1) * nodes, :] = value[:, lanes]
    stores.start(core_sums, send_upper_ref.at[pl.ds(send_lower_ref.shape[0], 2 * part)])
    put(weights, 4 * feat, inner_dot(node_x[...], node_pre_grad[...]))
    put(weights, 6 * feat, inner_dot(node_act[...], node_lin_grad[...]))
    put(weights, 3 * feat, inner_dot(act[...], lin_grad[...]))
    give(0, keep_upper_ref, send_upper_ref)
    high_part, low_part = split_parts(taken)
    put(weights, 2 * feat, inner_dot(latent, high_part) + inner_dot(latent, low_part))
    put(weights, feat, inner_dot(picked[...], pre_grad[...]))
    for copy in fifth:
        copy.wait()
    put(weights, 0, flat_dot(edge_t[...], pre_grad[...]))
    give(1, keep_lower_ref, send_lower_ref)
    local_ref[...] = (
        node_cot[...].astype(F32)
        + outer_dot(node_pre_grad[...], node_in[0:feat, :])
        + (outer_dot(high_part, w_recv[...]) + outer_dot(low_part, w_recv[...]))
    )
    stores.finish()


def edge_grad_kernel(
    receiver_hbm,
    pre_grad_hbm,
    edge_cot_hbm,
    w_hbm,
    agg_parts_hbm,
    out_hbm,
    receiver,
    pre_grad,
    edge_cot,
    w_edge,
    agg_parts,
    work,
    out,
    in_sems,
    out_sems,
):
    loads, stores = Copies(in_sems), Copies(out_sems)
    for source, target in (
        (receiver_hbm, receiver),
        (agg_parts_hbm, agg_parts),
        (w_hbm.at[0 : w_edge.shape[0]], w_edge),
        (pre_grad_hbm, pre_grad),
        (edge_cot_hbm, edge_cot),
    ):
        loads.start(source, target)
    loads.finish()
    column = as_column(receiver[...])
    for at in range(0, out.shape[0], ROWS):
        rows = slice(at, at + ROWS)
        hot = hot_rows(column[rows], agg_parts.shape[0] // 2)
        work[rows, :] = flat_dot(jnp.concatenate([hot, hot], 1), agg_parts[...]) + outer_dot(
            pre_grad[rows, :], w_edge[...]
        )
        for start in range(at, at + ROWS, CHUNK):
            c = slice(start, start + CHUNK)
            out[c, :] = (edge_cot[c, :].astype(F32) + work[c, :]).astype(BF16)
        stores.start(out.at[rows], out_hbm.at[rows])
    stores.finish()


def node_kernel(
    where_ref,
    from_ref,
    cut_ref,
    w_send_ref,
    local_ref,
    total_ref,
    first_ref,
    second_ref,
    stay_ref,
    slot_ref,
    ends,
):
    nodes, feat = local_ref.shape
    halo = first_ref.shape[0]
    width = total_ref.shape[1]
    turn = pl.multiple_of(where_ref[2], halo)
    ends[pl.ds(turn, halo), :] = first_ref[...]
    ends[pl.ds(halo - turn, halo), :] = second_ref[...]
    value = jnp.concatenate(
        [total_ref[block * nodes : (block + 1) * nodes, :] for block in range(feat // width)], 1
    )
    value = value + flat_dot(hot_columns(cut_ref[...], nodes), ends[...])
    high_part, low_part = split_parts(value)
    w_send = w_send_ref[...]
    grad = local_ref[...] + (outer_dot(high_part, w_send) + outer_dot(low_part, w_send))
    grad = grad.astype(BF16)
    where = from_ref[...]
    slot_ref[...] = flat_dot(hot_columns(where, slot_ref.shape[0], nodes), grad).astype(BF16)
    stay_ref[...] = flat_dot(hot_columns(where, nodes), grad).astype(BF16)


def back_kernel(pick_ref, stay_ref, came_ref, out_hbm, out, out_sems):
    stores = Copies(out_sems)
    hot = hot_columns(pick_ref[...], stay_ref.shape[0])
    out[...] = (stay_ref[...].astype(F32) + flat_dot(hot, came_ref[...])).astype(BF16)
    stores.start(out, out_hbm)
    stores.finish()


def flip(values, axis, mask):
    count = lax.axis_size(axis)
    return lax.ppermute(values, axis, [(i, i ^ mask) for i in range(count)])


def meet(values, axis, step):
    count = lax.axis_size(axis)
    pairs = [(i, (i + (step if i % 2 == 0 else -step)) % count) for i in range(count)]
    return lax.ppermute(values, axis, pairs)


def axis_bits(axis):
    return [(axis, b) for b in range(lax.axis_size(axis).bit_length() - 1)]


def exchange_orders():
    cross, dom_bits = axis_bits("tile")[1:], axis_bits("dom")
    side, line = dom_bits[:1], dom_bits[1:-1]
    return side + cross + line, line + side + cross


def after(values, *others):
    return lax.optimization_barrier((values, others))[0]


def total_of(values):
    return functools.reduce(jnp.add, [v.astype(F32) for v in values])


class Exchange:
    def __init__(self, values, count, order, relative):
        self.values = values
        self.count = count
        self.order = list(order)
        self.relative = relative
        self.outgoing = None

    def cut(self, *others):
        arrays = after(self.values, *others)
        self.count //= 2
        axis, bit = self.order[0]
        mine = (lax.axis_index(axis) >> bit) & 1

        def half(second):
            if self.relative:
                first = int(second) * self.count
                return total_of([a[first : first + self.count] for a in arrays]).astype(BF16)
            first = (mine if second else 1 - mine) * self.count
            return total_of(
                [lax.dynamic_slice_in_dim(a, first, self.count, 0) for a in arrays]
            ).astype(BF16)

        self.outgoing = half(False)
        self.values = [half(True)]
        return self.outgoing

    def send(self):
        axis, bit = self.order.pop(0)
        self.values.append(flip(self.outgoing, axis, 1 << bit))

    def total(self):
        return total_of(self.values)


def cut_all(parts, *others):
    return [part.cut(*others) for part in parts]


def send_all(parts):
    for part in parts:
        part.send()


def body(
    tile_latent,
    relay_pick,
    relay_from,
    cut_pick,
    edge_latent,
    edge_sender,
    edge_receiver,
    edge_in,
    edge_out,
    node_in,
    node_out,
    node_cot,
    edge_cot,
):
    nodes, feat = tile_latent.shape
    edges = edge_latent.shape[0]
    doms, tiles = lax.axis_size("dom"), lax.axis_size("tile")
    slots = relay_pick.shape[1]
    halo = cut_pick.shape[1] // 2
    table_rows = -(-(tiles * nodes + 2 * halo) // nodes) * nodes
    half, width = 7 * feat // 2, feat // tiles
    sds = jax.ShapeDtypeStruct
    node_bf16 = sds((nodes, feat), BF16)
    node_f32 = sds((nodes, feat), F32)
    edge_bf16 = sds((edges, feat), BF16)
    edge_f32 = sds((edges, feat), F32)
    slot_bf16 = sds((slots, feat), BF16)
    halo_bf16 = sds((halo, feat), BF16)
    square = sds((feat, feat), BF16)
    node_index = sds((nodes,), jnp.int32)
    edge_index = sds((edges,), jnp.int32)

    def exchange(rows):
        blocks = rows.reshape(doms, slots // doms, feat)
        return lax.all_to_all(blocks, "dom", split_axis=0, concat_axis=0, tiled=True).reshape(
            slots, feat
        )

    tile = lax.axis_index("tile")
    turn = jnp.where(lax.axis_index("dom") % 2 == 0, halo, 0)
    where = jnp.stack([tile & 1, tile, turn, lax.axis_index("dom")]).astype(jnp.int32)
    outgoing, pick_row = call(
        pick_kernel,
        "pick",
        [Kept(slot_bf16), Kept(relay_pick)],
        [relay_pick, tile_latent],
        [relay_pick, tile_latent, 2],
        limit=SMALL_LIMIT,
    )
    edge_t = jnp.transpose(after(edge_latent, outgoing))
    came = after(exchange(outgoing), edge_t)
    latent, first, second, from_row, cut_row = call(
        pool_kernel,
        "pool",
        [Kept(node_bf16), Kept(halo_bf16), Kept(halo_bf16)]
        + [Kept(sds((1, nodes), jnp.int32)), Kept(cut_pick)],
        [relay_from, cut_pick, tile_latent, Kept(came)],
        [node_index, cut_pick, node_bf16, sds((2 * halo, feat), BF16), 3],
        [where],
        SMALL_LIMIT,
    )
    far = flip(latent, "tile", 2)
    near = flip(latent, "tile", 1)
    first = meet(first, "dom", 1)
    second = meet(second, "dom", -1)
    base, w_send, w_out = call(
        base_kernel,
        "base",
        [Kept(edge_f32), Kept(square), Kept(square)],
        [edge_receiver, edge_latent, edge_in, edge_out, Kept(latent)],
        [edge_index, edge_bf16, square, square, 6],
    )
    across = flip(after(far, first, second, base), "tile", 1)

    orders = exchange_orders()
    rows = 7 * feat // doms
    bits = len(orders[0])
    fine = rows % 16 == 0
    span = tiles * half // 2
    places = [(order if fine else None, low) for order, low in zip(orders, (half, 0))]
    copies = 2 * sum(1 << len(order) if fine else tiles // 2 for order in orders)
    sum_rows = tiles * nodes
    (
        node_new,
        edge_new,
        pre_grad,
        agg_parts,
        local,
        keep_upper,
        keep_lower,
        send_upper,
        send_lower,
        own,
        opposite,
        back_first,
        back_second,
    ) = call(
        functools.partial(block_kernel, places),
        "block",
        [node_bf16, edge_bf16, edge_bf16, sds((2 * nodes, feat), BF16), Kept(node_f32)]
        + [sds((span, width), BF16)] * 2
        + [sds((span + 2 * sum_rows, width), BF16), sds((span, width), BF16)]
        + [Kept(sds((sum_rows, width), F32)), Kept(sds((sum_rows, width), BF16))]
        + [Kept(halo_bf16)] * 2,
        [edge_sender, edge_receiver]
        + [Kept(array) for array in (latent, near, far, across, first, second)]
        + [Kept(base), Kept(w_send), Kept(w_out)]
        + [edge_latent, edge_t, edge_in, node_in, node_out, node_cot, edge_cot],
        [edge_index, edge_index, sds((table_rows, feat), BF16), edge_bf16]
        + [sds((feat, edges), BF16), edge_bf16, square, sds((nodes, 2 * feat), BF16)]
        + [node_in, node_out, node_cot, edge_cot]
        + [node_bf16] * 4
        + [sds((2 * nodes, feat), BF16), node_f32, node_f32]
        + [edge_bf16] * 4
        + [edge_f32] * 3
        + [sds((edges, 1), F32), edge_f32, edge_f32]
        + [sds((tiles, 2 * half, width), BF16), sds((table_rows, feat), F32)]
        + [sds((2 * sum_rows, width), BF16)]
        + [9, 5 + copies],
        [where],
    )
    got_upper = flip(send_upper, "tile", 1)
    got_lower = flip(send_lower, "tile", 1)
    back_first = meet(back_first, "dom", 1)
    back_second = meet(back_second, "dom", -1)
    leaving = (opposite.astype(F32) + got_upper[span + sum_rows :].astype(F32)).astype(BF16)
    across = flip(leaving, "tile", 2)
    parts = []
    for order, keep, got in zip(
        orders, (keep_upper, keep_lower), (got_upper, got_lower), strict=True
    ):
        if fine:
            parts.append(Exchange([keep, got], span, order, True))
            continue
        labels = axis_bits("tile")[:0:-1] + axis_bits("dom")[-2::-1]
        axes = [labels.index(label) for label in order] + [bits, bits + 1]
        values = [
            jnp.transpose(whole.reshape([2] * bits + [rows, width]), axes)
            for whole in (keep, got[:span])
        ]
        parts.append(Exchange([v.reshape(span, width) for v in values], span, order, False))
    sent = parts[0].cut(leaving)
    parts[0].send()
    sent = parts[1].cut(sent, back_first, back_second, across)
    parts[1].send()
    total = own + got_upper[span : span + sum_rows].astype(F32) + across.astype(F32)
    stay, slot_grad = call(
        node_kernel,
        "node",
        [Kept(node_bf16), Kept(slot_bf16)],
        [Kept(array) for array in (from_row, cut_row, w_send, after(local, sent), total)]
        + [Kept(back_first), Kept(back_second)],
        [sds((2 * halo, feat), BF16)],
        [where],
        SMALL_LIMIT,
    )
    back_rows = exchange(slot_grad)
    sent = cut_all(parts, slot_grad)
    send_all(parts)
    [latent_grad] = call(
        back_kernel,
        "back",
        [node_bf16],
        [Kept(pick_row), Kept(stay), Kept(after(back_rows, *sent))],
        [node_bf16, 1],
        limit=SMALL_LIMIT,
    )
    [edge_grad] = call(
        edge_grad_kernel,
        "edge_grad",
        [edge_bf16],
        [edge_receiver, after(pre_grad, latent_grad), edge_cot, edge_in, agg_parts],
        [edge_index, edge_bf16, edge_bf16, square, sds((2 * nodes, feat), BF16)]
        + [edge_f32, edge_bf16, 5, edges // ROWS],
        limit=2 * SMALL_LIMIT,
    )
    first = edge_grad
    while parts[0].order:
        cut_all(parts, first)
        send_all(parts)
        first = ()
    top = axis_bits("dom")[-1][1]
    upper = (lax.axis_index("dom") >> top) & 1
    above, below = [part.total() for part in parts]
    sent = jnp.where(upper == 1, below, above).astype(BF16)
    kept = jnp.where(upper == 1, above, below)
    weight_shard = kept + flip(sent, "dom", 1 << top).astype(F32)
    return (node_new, edge_new, latent_grad, edge_grad, weight_shard)


def solution(mesh):
    rows = P(("dom", "tile"), None)
    flat = P(("dom", "tile"))
    in_specs = (rows, rows, flat, rows, rows, flat, flat, P(), P(), P(), P(), rows, rows)
    out_specs = (rows, rows, rows, rows, P("dom", "tile"))
    return jax.shard_map(body, mesh=mesh, in_specs=in_specs, out_specs=out_specs, check_vma=False)
```

```python
import functools

import jax
import jax.numpy as jnp
from jax import lax
from jax.experimental import pallas as pl
from jax.experimental.pallas import tpu as pltpu
from jax.sharding import PartitionSpec as P

EPSILON = 1e-05
BF16 = jnp.bfloat16
F32 = jnp.float32
ROWS = 256
CHUNK = 32
VMEM_LIMIT = 30 * 1024 * 1024
SMALL_LIMIT = 8 * 1024 * 1024


def layer_norm(values):
    center = values - jnp.mean(values, -1, keepdims=True)
    inverse = lax.rsqrt(jnp.mean(center * center, -1, keepdims=True) + EPSILON)
    return (center * inverse, inverse)


def norm_grad(normed, inverse, upstream):
    mean_up = jnp.mean(upstream, -1, keepdims=True)
    mean_cross = jnp.mean(upstream * normed, -1, keepdims=True)
    return inverse * (upstream - mean_up - normed * mean_cross)


def silu_pair(values):
    sigmoid = 0.5 * jnp.tanh(0.5 * values) + 0.5
    return values * sigmoid, sigmoid * (1.0 + values * (1.0 - sigmoid))


def flat_dot(left_mat, right_mat):
    return jnp.dot(left_mat, right_mat, preferred_element_type=F32)


def inner_dot(left_mat, right_mat):
    return lax.dot_general(
        left_mat, right_mat, (((0,), (0,)), ((), ())), preferred_element_type=F32
    )


def outer_dot(left_mat, right_mat):
    return lax.dot_general(
        left_mat, right_mat, (((1,), (1,)), ((), ())), preferred_element_type=F32
    )


def split_parts(values):
    high_part = values.astype(BF16)
    return high_part, (values - high_part.astype(F32)).astype(BF16)


def marks(hits):
    return jnp.where(hits, 1.0, 0.0).astype(BF16)


def hot_columns(index_row, count, first=0):
    shape = (count, index_row.shape[-1])
    at = lax.broadcasted_iota(jnp.int32, shape, 0) + first
    return marks(jnp.broadcast_to(index_row.reshape(1, -1), shape) == at)


def as_column(index_row):
    shape = (128, index_row.shape[-1])
    return jnp.transpose(jnp.broadcast_to(index_row.reshape(1, -1), shape))


def hot_rows(index_column, count):
    at = lax.broadcasted_iota(jnp.int32, index_column.shape, 1)
    return jnp.concatenate(
        [marks(index_column == at + 128 * k) for k in range(count // 128)], 1
    )


class Kept:
    def __init__(self, array):
        self.array = array


def call(kernel, name, outs, ins, scratch, scalars=(), limit=VMEM_LIMIT):
    def spec(array):
        return pl.BlockSpec(memory_space=pltpu.VMEM if isinstance(array, Kept) else pltpu.HBM)

    def placed(array):
        if isinstance(array, Kept):
            return array.array
        return pltpu.with_memory_space_constraint(array, pltpu.HBM)

    shapes = [
        pltpu.SemaphoreType.DMA((s,)) if isinstance(s, int) else pltpu.VMEM(s.shape, s.dtype)
        for s in scratch
    ]
    return pl.pallas_call(
        kernel,
        out_shape=[
            array.array if isinstance(array, Kept) else pltpu.HBM(array.shape, array.dtype)
            for array in outs
        ],
        in_specs=[pl.BlockSpec(memory_space=pltpu.SMEM)] * len(scalars) + [spec(a) for a in ins],
        out_specs=[spec(array) for array in outs],
        scratch_shapes=shapes,
        compiler_params=pltpu.CompilerParams(vmem_limit_bytes=limit),
        name=name,
    )(*scalars, *[placed(array) for array in ins])


class Copies:
    def __init__(self, sems):
        self.sems = sems
        self.made = 0
        self.open = []

    def start(self, source, target):
        copy = pltpu.make_async_copy(source, target, self.sems.at[self.made])
        copy.start()
        self.made += 1
        self.open.append(copy)
        return copy

    def finish(self):
        for copy in self.open:
            copy.wait()


def pick_kernel(pick_hbm, tile_hbm, out_ref, pick_ref, pick, tile, in_sems):
    loads = Copies(in_sems)
    loads.start(pick_hbm, pick)
    loads.start(tile_hbm, tile)
    loads.finish()
    pick_ref[...] = pick[...]
    rows = hot_rows(as_column(pick[...]), tile.shape[0])
    out_ref[...] = flat_dot(rows, tile[...]).astype(BF16)


def pool_kernel(
    where_ref,
    from_hbm,
    cut_hbm,
    tile_hbm,
    came_ref,
    latent_ref,
    first_ref,
    second_ref,
    from_ref,
    cut_ref,
    at,
    cut,
    tile,
    ends,
    in_sems,
):
    loads = Copies(in_sems)
    for source, target in ((from_hbm, at), (cut_hbm, cut), (tile_hbm, tile)):
        loads.start(source, target)
    loads.finish()
    from_ref[...] = at[...].reshape(from_ref.shape)
    cut_ref[...] = cut[...]
    nodes = tile.shape[0]
    halo = first_ref.shape[0]
    rows = hot_rows(as_column(at[...]), nodes + came_ref.shape[0])
    value = flat_dot(rows[:, :nodes], tile[...]) + flat_dot(rows[:, nodes:], came_ref[...])
    value = value.astype(BF16)
    latent_ref[...] = value
    ends[...] = inner_dot(hot_columns(cut[...], nodes), value).astype(BF16)
    turn = pl.multiple_of(where_ref[2], halo)
    first_ref[...] = ends[pl.ds(turn, halo), :]
    second_ref[...] = ends[pl.ds(halo - turn, halo), :]


def base_kernel(
    receiver_hbm,
    edge_hbm,
    edge_in_hbm,
    edge_out_hbm,
    latent_ref,
    base_ref,
    w_send_ref,
    edge_out_ref,
    receiver,
    edge_lat,
    w_edge,
    w_recv,
    in_sems,
):
    feat = edge_out_ref.shape[0]
    loads = Copies(in_sems)
    first = [
        loads.start(receiver_hbm, receiver),
        loads.start(edge_hbm, edge_lat),
        loads.start(edge_in_hbm.at[0:feat], w_edge),
        loads.start(edge_in_hbm.at[2 * feat : 3 * feat], w_recv),
    ]
    second = [
        loads.start(edge_in_hbm.at[feat : 2 * feat], w_send_ref),
        loads.start(edge_out_hbm, edge_out_ref),
    ]
    for copy in first:
        copy.wait()
    column = as_column(receiver[...])
    latent = latent_ref[...]
    for at in range(0, edge_lat.shape[0], ROWS):
        rows = slice(at, at + ROWS)
        taken = flat_dot(hot_rows(column[rows], latent.shape[0]), latent).astype(BF16)
        base_ref[rows, :] = flat_dot(edge_lat[rows, :], w_edge[...]) + flat_dot(taken, w_recv[...])
    for copy in second:
        copy.wait()


def put(weights, first, terms):
    for t in range(terms.shape[1] // 128):
        weights[t, first : first + terms.shape[0], :] = terms[:, t * 128 : (t + 1) * 128].astype(
            BF16
        )


def block_kernel(
    places,
    where_ref,
    sender_hbm,
    receiver_hbm,
    latent_ref,
    near_ref,
    far_ref,
    cross_ref,
    first_ref,
    second_ref,
    base_ref,
    w_send,
    edge_out,
    edge_hbm,
    edge_t_hbm,
    w_recv_hbm,
    node_in_hbm,
    node_out_hbm,
    node_cot_hbm,
    edge_cot_hbm,
    node_new_hbm,
    edge_new_hbm,
    pre_grad_hbm,
    agg_parts_hbm,
    local_ref,
    keep_upper_ref,
    keep_lower_ref,
    send_upper_ref,
    send_lower_ref,
    own_ref,
    opposite_ref,
    back_first_ref,
    back_second_ref,
    sender,
    receiver,
    table,
    edge_lat,
    edge_t,
    picked,
    w_recv,
    node_x,
    node_in,
    node_out,
    node_cot,
    edge_cot,
    node_new,
    node_act,
    node_lin_grad,
    node_pre_grad,
    agg_parts,
    node_work,
    node_slope,
    edge_new,
    act,
    lin_grad,
    pre_grad,
    work,
    slope,
    normed,
    inverse,
    edge_up,
    back_work,
    weights,
    sums,
    core_sums,
    in_sems,
    out_sems,
):
    feat = edge_out.shape[0]
    nodes = node_cot.shape[0]
    edges = edge_lat.shape[0]
    halo = first_ref.shape[0]
    tiles, _, width = weights.shape
    core = where_ref[0]
    tile = where_ref[1]
    turn = pl.multiple_of(where_ref[2], halo)
    part = tiles * nodes
    held = part + 2 * halo
    loads = Copies(in_sems)
    stores = Copies(out_sems)

    def rows_of(mask):
        return pl.ds(pl.multiple_of((tile ^ mask) * nodes, nodes), nodes)

    first = [
        loads.start(sender_hbm, sender),
        loads.start(receiver_hbm, receiver),
    ]
    second = [loads.start(edge_hbm, edge_lat)]
    third = [
        loads.start(node_in_hbm, node_in),
        loads.start(node_out_hbm, node_out),
        loads.start(node_cot_hbm, node_cot),
    ]
    fourth = [loads.start(edge_cot_hbm, edge_cot)]
    fifth = [
        loads.start(edge_t_hbm, edge_t),
        loads.start(w_recv_hbm.at[2 * feat : 3 * feat], w_recv),
    ]

    for mask, ref in enumerate((latent_ref, near_ref, far_ref, cross_ref)):
        table[rows_of(mask), :] = ref[...]
    table[pl.ds(part + turn, halo), :] = first_ref[...]
    table[pl.ds(part + halo - turn, halo), :] = second_ref[...]
    table[held:, :] = jnp.zeros((table.shape[0] - held, feat), BF16)
    for copy in first:
        copy.wait()
    latent = latent_ref[...]
    node_x[:, 0:feat] = latent
    sender_column = as_column(sender[...])
    receiver_hot = hot_rows(as_column(receiver[...]), nodes)
    receiver_rows = hot_columns(receiver[...], nodes)
    blocks = [slice(at, at + ROWS) for at in range(0, edges, ROWS)]

    def chunks(rows):
        return [slice(at, at + CHUNK) for at in range(rows.start, rows.stop, CHUNK)]

    for rows in blocks:
        hot = hot_rows(sender_column[rows], table.shape[0])
        picked[rows, :] = flat_dot(hot, table[...]).astype(BF16)
    for rows in blocks:
        work[rows, :] = flat_dot(picked[rows, :], w_send[...])
        for c in chunks(rows):
            value, slope[c, :] = silu_pair(base_ref[c, :] + work[c, :])
            act[c, :] = value.astype(BF16)
        normed[rows, :] = flat_dot(act[rows, :], edge_out[...])
        if rows.start == 0:
            for copy in second:
                copy.wait()
        for c in chunks(rows):
            value, scale = layer_norm(normed[c, :])
            normed[c, :] = value
            inverse[c, :] = scale
            edge_new[c, :] = (edge_lat[c, :].astype(F32) + value).astype(BF16)
    stores.start(edge_new, edge_new_hbm)
    node_x[:, feat:] = flat_dot(receiver_rows, edge_new[...]).astype(BF16)

    for copy in third:
        copy.wait()
    node_rows = slice(0, nodes)
    node_work[...] = flat_dot(node_x[...], node_in[...])
    for c in chunks(node_rows):
        value, node_slope[c, :] = silu_pair(node_work[c, :])
        node_act[c, :] = value.astype(BF16)
    node_work[...] = flat_dot(node_act[...], node_out[...])
    for c in chunks(node_rows):
        value, scale = layer_norm(node_work[c, :])
        node_new[c, :] = (node_x[c, 0:feat].astype(F32) + value).astype(BF16)
        up = node_cot[c, :].astype(F32)
        node_lin_grad[c, :] = norm_grad(value, scale, up).astype(BF16)
    stores.start(node_new, node_new_hbm)
    node_work[...] = outer_dot(node_lin_grad[...], node_out[...])
    for c in chunks(node_rows):
        node_pre_grad[c, :] = (node_work[c, :] * node_slope[c, :]).astype(BF16)
    node_work[...] = outer_dot(node_pre_grad[...], node_in[feat:, :])
    for c in chunks(node_rows):
        agg_parts[c, :], low_part = split_parts(node_work[c, :])
        agg_parts[slice(c.start + nodes, c.stop + nodes), :] = low_part
    stores.start(agg_parts, agg_parts_hbm)

    for copy in fourth:
        copy.wait()
    for rows in blocks:
        hot = receiver_hot[rows]
        edge_up[rows, :] = flat_dot(jnp.concatenate([hot, hot], 1), agg_parts[...])
        for c in chunks(rows):
            up = edge_cot[c, :].astype(F32) + edge_up[c, :]
            edge_up[c, :] = up
            lin_grad[c, :] = norm_grad(normed[c, :], inverse[c, :], up).astype(BF16)
        back_work[rows, :] = outer_dot(lin_grad[rows, :], edge_out[...])
        for c in chunks(rows):
            pre_grad[c, :] = (back_work[c, :] * slope[c, :]).astype(BF16)
    stores.start(pre_grad, pre_grad_hbm)
    taken = flat_dot(receiver_rows, pre_grad[...])

    def give(which, keep_ref, send_ref):
        order, low = places[which]
        half = keep_ref.shape[0] // (tiles // 2)
        if order is None:
            for upper in range(tiles // 2):
                to = pl.ds(upper * half, half)
                rows = slice(low, low + half)
                stores.start(weights.at[2 * upper + core, rows], keep_ref.at[to])
                stores.start(weights.at[2 * upper + 1 - core, rows], send_ref.at[to])
            return
        here = {"tile": tile, "dom": where_ref[3]}
        rows = keep_ref.shape[0] >> len(order)
        for index in range(1 << len(order)):
            upper = block = 0
            for at, (axis, bit) in enumerate(order):
                flipped = 1 - ((index >> (len(order) - 1 - at)) & 1)
                value = ((here[axis] >> bit) & 1) ^ flipped
                if axis == "tile":
                    upper = upper + (value << (bit - 1))
                else:
                    block = block + (value << bit)
            source = pl.ds(pl.multiple_of(low + block * rows, 16), rows)
            to = pl.ds(index * rows, rows)
            stores.start(weights.at[2 * upper + core, source], keep_ref.at[to])
            stores.start(weights.at[2 * upper + 1 - core, source], send_ref.at[to])

    part_rows = sums.shape[0] // 2
    for start in (0, part_rows):
        sums[start : start + part_rows, :] = flat_dot(
            hot_columns(sender[...], part_rows, start), pre_grad[...]
        )
    back_first_ref[...] = sums[pl.ds(part + turn, halo), :].astype(BF16)
    back_second_ref[...] = sums[pl.ds(part + halo - turn, halo), :].astype(BF16)
    for mask, ref, first in (
        (0, own_ref, 0),
        (2, opposite_ref, 0),
        (1, core_sums, 0),
        (3, core_sums, part),
    ):
        value = sums[rows_of(mask), :].astype(ref.dtype)
        for at in range(tiles):
            lanes = slice(at * width, (at + 1) * width)
            ref[first + at * nodes : first + (at + 1) * nodes, :] = value[:, lanes]
    stores.start(core_sums, send_upper_ref.at[pl.ds(send_lower_ref.shape[0], 2 * part)])
    put(weights, 4 * feat, inner_dot(node_x[...], node_pre_grad[...]))
    put(weights, 6 * feat, inner_dot(node_act[...], node_lin_grad[...]))
    put(weights, 3 * feat, inner_dot(act[...], lin_grad[...]))
    give(0, keep_upper_ref, send_upper_ref)
    high_part, low_part = split_parts(taken)
    put(weights, 2 * feat, inner_dot(latent, high_part) + inner_dot(latent, low_part))
    put(weights, feat, inner_dot(picked[...], pre_grad[...]))
    for copy in fifth:
        copy.wait()
    put(weights, 0, flat_dot(edge_t[...], pre_grad[...]))
    give(1, keep_lower_ref, send_lower_ref)
    local_ref[...] = (
        node_cot[...].astype(F32)
        + outer_dot(node_pre_grad[...], node_in[0:feat, :])
        + (outer_dot(high_part, w_recv[...]) + outer_dot(low_part, w_recv[...]))
    )
    stores.finish()


def edge_grad_kernel(
    receiver_hbm,
    pre_grad_hbm,
    edge_cot_hbm,
    w_hbm,
    agg_parts_hbm,
    out_hbm,
    receiver,
    pre_grad,
    edge_cot,
    w_edge,
    agg_parts,
    work,
    out,
    in_sems,
    out_sems,
):
    loads, stores = Copies(in_sems), Copies(out_sems)
    for source, target in (
        (receiver_hbm, receiver),
        (agg_parts_hbm, agg_parts),
        (w_hbm.at[0 : w_edge.shape[0]], w_edge),
        (pre_grad_hbm, pre_grad),
        (edge_cot_hbm, edge_cot),
    ):
        loads.start(source, target)
    loads.finish()
    column = as_column(receiver[...])
    for at in range(0, out.shape[0], ROWS):
        rows = slice(at, at + ROWS)
        hot = hot_rows(column[rows], agg_parts.shape[0] // 2)
        work[rows, :] = flat_dot(jnp.concatenate([hot, hot], 1), agg_parts[...]) + outer_dot(
            pre_grad[rows, :], w_edge[...]
        )
        for start in range(at, at + ROWS, CHUNK):
            c = slice(start, start + CHUNK)
            out[c, :] = (edge_cot[c, :].astype(F32) + work[c, :]).astype(BF16)
        stores.start(out.at[rows], out_hbm.at[rows])
    stores.finish()


def node_kernel(
    where_ref,
    from_ref,
    cut_ref,
    w_send_ref,
    local_ref,
    total_ref,
    first_ref,
    second_ref,
    stay_ref,
    slot_ref,
    ends,
):
    nodes, feat = local_ref.shape
    halo = first_ref.shape[0]
    width = total_ref.shape[1]
    turn = pl.multiple_of(where_ref[2], halo)
    ends[pl.ds(turn, halo), :] = first_ref[...]
    ends[pl.ds(halo - turn, halo), :] = second_ref[...]
    value = jnp.concatenate(
        [total_ref[block * nodes : (block + 1) * nodes, :] for block in range(feat // width)], 1
    )
    value = value + flat_dot(hot_columns(cut_ref[...], nodes), ends[...])
    high_part, low_part = split_parts(value)
    w_send = w_send_ref[...]
    grad = local_ref[...] + (outer_dot(high_part, w_send) + outer_dot(low_part, w_send))
    grad = grad.astype(BF16)
    where = from_ref[...]
    slot_ref[...] = flat_dot(hot_columns(where, slot_ref.shape[0], nodes), grad).astype(BF16)
    stay_ref[...] = flat_dot(hot_columns(where, nodes), grad).astype(BF16)


def back_kernel(pick_ref, stay_ref, came_ref, out_hbm, out, out_sems):
    stores = Copies(out_sems)
    hot = hot_columns(pick_ref[...], stay_ref.shape[0])
    out[...] = (stay_ref[...].astype(F32) + flat_dot(hot, came_ref[...])).astype(BF16)
    stores.start(out, out_hbm)
    stores.finish()


def flip(values, axis, mask):
    count = lax.axis_size(axis)
    return lax.ppermute(values, axis, [(i, i ^ mask) for i in range(count)])


def meet(values, axis, step):
    count = lax.axis_size(axis)
    pairs = [(i, (i + (step if i % 2 == 0 else -step)) % count) for i in range(count)]
    return lax.ppermute(values, axis, pairs)


def axis_bits(axis):
    return [(axis, b) for b in range(lax.axis_size(axis).bit_length() - 1)]


def exchange_orders():
    cross, dom_bits = axis_bits("tile")[1:], axis_bits("dom")
    side, line = dom_bits[:1], dom_bits[1:-1]
    return cross + side + line, line + cross + side


def after(values, *others):
    return lax.optimization_barrier((values, others))[0]


def total_of(values):
    return functools.reduce(jnp.add, [v.astype(F32) for v in values])


class Exchange:
    def __init__(self, values, count, order, relative):
        self.values = values
        self.count = count
        self.order = list(order)
        self.relative = relative
        self.outgoing = None

    def cut(self, *others):
        arrays = after(self.values, *others)
        self.count //= 2
        axis, bit = self.order[0]
        mine = (lax.axis_index(axis) >> bit) & 1

        def half(second):
            if self.relative:
                first = int(second) * self.count
                return total_of([a[first : first + self.count] for a in arrays]).astype(BF16)
            first = (mine if second else 1 - mine) * self.count
            return total_of(
                [lax.dynamic_slice_in_dim(a, first, self.count, 0) for a in arrays]
            ).astype(BF16)

        self.outgoing = half(False)
        self.values = [half(True)]
        return self.outgoing

    def send(self):
        axis, bit = self.order.pop(0)
        self.values.append(flip(self.outgoing, axis, 1 << bit))

    def total(self):
        return total_of(self.values)


def cut_all(parts, *others):
    return [part.cut(*others) for part in parts]


def send_all(parts):
    for part in parts:
        part.send()


def body(
    tile_latent,
    relay_pick,
    relay_from,
    cut_pick,
    edge_latent,
    edge_sender,
    edge_receiver,
    edge_in,
    edge_out,
    node_in,
    node_out,
    node_cot,
    edge_cot,
):
    nodes, feat = tile_latent.shape
    edges = edge_latent.shape[0]
    doms, tiles = lax.axis_size("dom"), lax.axis_size("tile")
    slots = relay_pick.shape[1]
    halo = cut_pick.shape[1] // 2
    table_rows = -(-(tiles * nodes + 2 * halo) // nodes) * nodes
    half, width = 7 * feat // 2, feat // tiles
    sds = jax.ShapeDtypeStruct
    node_bf16 = sds((nodes, feat), BF16)
    node_f32 = sds((nodes, feat), F32)
    edge_bf16 = sds((edges, feat), BF16)
    edge_f32 = sds((edges, feat), F32)
    slot_bf16 = sds((slots, feat), BF16)
    halo_bf16 = sds((halo, feat), BF16)
    square = sds((feat, feat), BF16)
    node_index = sds((nodes,), jnp.int32)
    edge_index = sds((edges,), jnp.int32)

    def exchange(rows):
        blocks = rows.reshape(doms, slots // doms, feat)
        return lax.all_to_all(blocks, "dom", split_axis=0, concat_axis=0, tiled=True).reshape(
            slots, feat
        )

    tile = lax.axis_index("tile")
    turn = jnp.where(lax.axis_index("dom") % 2 == 0, halo, 0)
    where = jnp.stack([tile & 1, tile, turn, lax.axis_index("dom")]).astype(jnp.int32)
    outgoing, pick_row = call(
        pick_kernel,
        "pick",
        [Kept(slot_bf16), Kept(relay_pick)],
        [relay_pick, tile_latent],
        [relay_pick, tile_latent, 2],
        limit=SMALL_LIMIT,
    )
    edge_t = jnp.transpose(after(edge_latent, outgoing))
    came = after(exchange(outgoing), edge_t)
    latent, first, second, from_row, cut_row = call(
        pool_kernel,
        "pool",
        [Kept(node_bf16), Kept(halo_bf16), Kept(halo_bf16)]
        + [Kept(sds((1, nodes), jnp.int32)), Kept(cut_pick)],
        [relay_from, cut_pick, tile_latent, Kept(came)],
        [node_index, cut_pick, node_bf16, sds((2 * halo, feat), BF16), 3],
        [where],
        SMALL_LIMIT,
    )
    far = flip(latent, "tile", 2)
    near = flip(latent, "tile", 1)
    first = meet(first, "dom", 1)
    second = meet(second, "dom", -1)
    base, w_send, w_out = call(
        base_kernel,
        "base",
        [Kept(edge_f32), Kept(square), Kept(square)],
        [edge_receiver, edge_latent, edge_in, edge_out, Kept(latent)],
        [edge_index, edge_bf16, square, square, 6],
    )
    across = flip(after(far, first, second, base), "tile", 1)

    orders = exchange_orders()
    rows = 7 * feat // doms
    bits = len(orders[0])
    fine = rows % 16 == 0
    span = tiles * half // 2
    places = [(order if fine else None, low) for order, low in zip(orders, (half, 0))]
    copies = 2 * sum(1 << len(order) if fine else tiles // 2 for order in orders)
    sum_rows = tiles * nodes
    (
        node_new,
        edge_new,
        pre_grad,
        agg_parts,
        local,
        keep_upper,
        keep_lower,
        send_upper,
        send_lower,
        own,
        opposite,
        back_first,
        back_second,
    ) = call(
        functools.partial(block_kernel, places),
        "block",
        [node_bf16, edge_bf16, edge_bf16, sds((2 * nodes, feat), BF16), Kept(node_f32)]
        + [sds((span, width), BF16)] * 2
        + [sds((span + 2 * sum_rows, width), BF16), sds((span, width), BF16)]
        + [Kept(sds((sum_rows, width), F32)), Kept(sds((sum_rows, width), BF16))]
        + [Kept(halo_bf16)] * 2,
        [edge_sender, edge_receiver]
        + [Kept(array) for array in (latent, near, far, across, first, second)]
        + [Kept(base), Kept(w_send), Kept(w_out)]
        + [edge_latent, edge_t, edge_in, node_in, node_out, node_cot, edge_cot],
        [edge_index, edge_index, sds((table_rows, feat), BF16), edge_bf16]
        + [sds((feat, edges), BF16), edge_bf16, square, sds((nodes, 2 * feat), BF16)]
        + [node_in, node_out, node_cot, edge_cot]
        + [node_bf16] * 4
        + [sds((2 * nodes, feat), BF16), node_f32, node_f32]
        + [edge_bf16] * 4
        + [edge_f32] * 3
        + [sds((edges, 1), F32), edge_f32, edge_f32]
        + [sds((tiles, 2 * half, width), BF16), sds((table_rows, feat), F32)]
        + [sds((2 * sum_rows, width), BF16)]
        + [9, 5 + copies],
        [where],
    )
    got_upper = flip(send_upper, "tile", 1)
    got_lower = flip(send_lower, "tile", 1)
    back_first = meet(back_first, "dom", 1)
    back_second = meet(back_second, "dom", -1)
    leaving = (opposite.astype(F32) + got_upper[span + sum_rows :].astype(F32)).astype(BF16)
    across = flip(leaving, "tile", 2)
    parts = []
    for order, keep, got in zip(
        orders, (keep_upper, keep_lower), (got_upper, got_lower), strict=True
    ):
        if fine:
            parts.append(Exchange([keep, got], span, order, True))
            continue
        labels = axis_bits("tile")[:0:-1] + axis_bits("dom")[-2::-1]
        axes = [labels.index(label) for label in order] + [bits, bits + 1]
        values = [
            jnp.transpose(whole.reshape([2] * bits + [rows, width]), axes)
            for whole in (keep, got[:span])
        ]
        parts.append(Exchange([v.reshape(span, width) for v in values], span, order, False))
    sent = parts[0].cut(leaving)
    parts[0].send()
    sent = parts[1].cut(sent, back_first, back_second, across)
    parts[1].send()
    total = own + got_upper[span : span + sum_rows].astype(F32) + across.astype(F32)
    stay, slot_grad = call(
        node_kernel,
        "node",
        [Kept(node_bf16), Kept(slot_bf16)],
        [Kept(array) for array in (from_row, cut_row, w_send, after(local, sent), total)]
        + [Kept(back_first), Kept(back_second)],
        [sds((2 * halo, feat), BF16)],
        [where],
        SMALL_LIMIT,
    )
    back_rows = exchange(slot_grad)
    [edge_grad] = call(
        edge_grad_kernel,
        "edge_grad",
        [edge_bf16],
        [edge_receiver, after(pre_grad, slot_grad), edge_cot, edge_in, agg_parts],
        [edge_index, edge_bf16, edge_bf16, square, sds((2 * nodes, feat), BF16)]
        + [edge_f32, edge_bf16, 5, edges // ROWS],
        limit=2 * SMALL_LIMIT,
    )
    sent = cut_all(parts, edge_grad)
    send_all(parts)
    [latent_grad] = call(
        back_kernel,
        "back",
        [node_bf16],
        [Kept(pick_row), Kept(stay), Kept(after(back_rows, *sent))],
        [node_bf16, 1],
        limit=SMALL_LIMIT,
    )
    first = latent_grad
    while parts[0].order:
        cut_all(parts, first)
        send_all(parts)
        first = ()
    top = axis_bits("dom")[-1][1]
    upper = (lax.axis_index("dom") >> top) & 1
    above, below = [part.total() for part in parts]
    sent = jnp.where(upper == 1, below, above).astype(BF16)
    kept = jnp.where(upper == 1, above, below)
    weight_shard = kept + flip(sent, "dom", 1 << top).astype(F32)
    return (node_new, edge_new, latent_grad, edge_grad, weight_shard)


def solution(mesh):
    rows = P(("dom", "tile"), None)
    flat = P(("dom", "tile"))
    in_specs = (rows, rows, flat, rows, rows, flat, flat, P(), P(), P(), P(), rows, rows)
    out_specs = (rows, rows, rows, rows, P("dom", "tile"))
    return jax.shard_map(body, mesh=mesh, in_specs=in_specs, out_specs=out_specs, check_vma=False)
```

```python
import functools

import jax
import jax.numpy as jnp
from jax import lax
from jax.experimental import pallas as pl
from jax.experimental.pallas import tpu as pltpu
from jax.sharding import PartitionSpec as P

EPSILON = 1e-05
BF16 = jnp.bfloat16
F32 = jnp.float32
ROWS = 256
CHUNK = 32
VMEM_LIMIT = 30 * 1024 * 1024
SMALL_LIMIT = 8 * 1024 * 1024


def layer_norm(values):
    center = values - jnp.mean(values, -1, keepdims=True)
    inverse = lax.rsqrt(jnp.mean(center * center, -1, keepdims=True) + EPSILON)
    return (center * inverse, inverse)


def norm_grad(normed, inverse, upstream):
    mean_up = jnp.mean(upstream, -1, keepdims=True)
    mean_cross = jnp.mean(upstream * normed, -1, keepdims=True)
    return inverse * (upstream - mean_up - normed * mean_cross)


def silu_pair(values):
    sigmoid = 0.5 * jnp.tanh(0.5 * values) + 0.5
    return values * sigmoid, sigmoid * (1.0 + values * (1.0 - sigmoid))


def flat_dot(left_mat, right_mat):
    return jnp.dot(left_mat, right_mat, preferred_element_type=F32)


def inner_dot(left_mat, right_mat):
    return lax.dot_general(
        left_mat, right_mat, (((0,), (0,)), ((), ())), preferred_element_type=F32
    )


def outer_dot(left_mat, right_mat):
    return lax.dot_general(
        left_mat, right_mat, (((1,), (1,)), ((), ())), preferred_element_type=F32
    )


def split_parts(values):
    high_part = values.astype(BF16)
    return high_part, (values - high_part.astype(F32)).astype(BF16)


def marks(hits):
    return jnp.where(hits, 1.0, 0.0).astype(BF16)


def hot_columns(index_row, count, first=0):
    shape = (count, index_row.shape[-1])
    at = lax.broadcasted_iota(jnp.int32, shape, 0) + first
    return marks(jnp.broadcast_to(index_row.reshape(1, -1), shape) == at)


def as_column(index_row):
    shape = (128, index_row.shape[-1])
    return jnp.transpose(jnp.broadcast_to(index_row.reshape(1, -1), shape))


def hot_rows(index_column, count):
    at = lax.broadcasted_iota(jnp.int32, index_column.shape, 1)
    return jnp.concatenate(
        [marks(index_column == at + 128 * k) for k in range(count // 128)], 1
    )


class Kept:
    def __init__(self, array):
        self.array = array


def call(kernel, name, outs, ins, scratch, scalars=(), limit=VMEM_LIMIT):
    def spec(array):
        return pl.BlockSpec(memory_space=pltpu.VMEM if isinstance(array, Kept) else pltpu.HBM)

    def placed(array):
        if isinstance(array, Kept):
            return array.array
        return pltpu.with_memory_space_constraint(array, pltpu.HBM)

    shapes = [
        pltpu.SemaphoreType.DMA((s,)) if isinstance(s, int) else pltpu.VMEM(s.shape, s.dtype)
        for s in scratch
    ]
    return pl.pallas_call(
        kernel,
        out_shape=[
            array.array if isinstance(array, Kept) else pltpu.HBM(array.shape, array.dtype)
            for array in outs
        ],
        in_specs=[pl.BlockSpec(memory_space=pltpu.SMEM)] * len(scalars) + [spec(a) for a in ins],
        out_specs=[spec(array) for array in outs],
        scratch_shapes=shapes,
        compiler_params=pltpu.CompilerParams(vmem_limit_bytes=limit),
        name=name,
    )(*scalars, *[placed(array) for array in ins])


class Copies:
    def __init__(self, sems):
        self.sems = sems
        self.made = 0
        self.open = []

    def start(self, source, target):
        copy = pltpu.make_async_copy(source, target, self.sems.at[self.made])
        copy.start()
        self.made += 1
        self.open.append(copy)
        return copy

    def finish(self):
        for copy in self.open:
            copy.wait()


def pick_kernel(pick_hbm, tile_hbm, out_ref, pick_ref, pick, tile, in_sems):
    loads = Copies(in_sems)
    loads.start(pick_hbm, pick)
    loads.start(tile_hbm, tile)
    loads.finish()
    pick_ref[...] = pick[...]
    rows = hot_rows(as_column(pick[...]), tile.shape[0])
    out_ref[...] = flat_dot(rows, tile[...]).astype(BF16)


def pool_kernel(
    where_ref,
    from_hbm,
    cut_hbm,
    tile_hbm,
    came_ref,
    latent_ref,
    first_ref,
    second_ref,
    from_ref,
    cut_ref,
    at,
    cut,
    tile,
    ends,
    in_sems,
):
    loads = Copies(in_sems)
    for source, target in ((from_hbm, at), (cut_hbm, cut), (tile_hbm, tile)):
        loads.start(source, target)
    loads.finish()
    from_ref[...] = at[...].reshape(from_ref.shape)
    cut_ref[...] = cut[...]
    nodes = tile.shape[0]
    halo = first_ref.shape[0]
    rows = hot_rows(as_column(at[...]), nodes + came_ref.shape[0])
    value = flat_dot(rows[:, :nodes], tile[...]) + flat_dot(rows[:, nodes:], came_ref[...])
    value = value.astype(BF16)
    latent_ref[...] = value
    ends[...] = inner_dot(hot_columns(cut[...], nodes), value).astype(BF16)
    turn = pl.multiple_of(where_ref[2], halo)
    first_ref[...] = ends[pl.ds(turn, halo), :]
    second_ref[...] = ends[pl.ds(halo - turn, halo), :]


def base_kernel(
    receiver_hbm,
    edge_hbm,
    edge_in_hbm,
    edge_out_hbm,
    latent_ref,
    base_ref,
    w_send_ref,
    edge_out_ref,
    receiver,
    edge_lat,
    w_edge,
    w_recv,
    in_sems,
):
    feat = edge_out_ref.shape[0]
    loads = Copies(in_sems)
    first = [
        loads.start(receiver_hbm, receiver),
        loads.start(edge_hbm, edge_lat),
        loads.start(edge_in_hbm.at[0:feat], w_edge),
        loads.start(edge_in_hbm.at[2 * feat : 3 * feat], w_recv),
    ]
    second = [
        loads.start(edge_in_hbm.at[feat : 2 * feat], w_send_ref),
        loads.start(edge_out_hbm, edge_out_ref),
    ]
    for copy in first:
        copy.wait()
    column = as_column(receiver[...])
    latent = latent_ref[...]
    for at in range(0, edge_lat.shape[0], ROWS):
        rows = slice(at, at + ROWS)
        taken = flat_dot(hot_rows(column[rows], latent.shape[0]), latent).astype(BF16)
        base_ref[rows, :] = flat_dot(edge_lat[rows, :], w_edge[...]) + flat_dot(taken, w_recv[...])
    for copy in second:
        copy.wait()


def put(weights, first, terms):
    for t in range(terms.shape[1] // 128):
        weights[t, first : first + terms.shape[0], :] = terms[:, t * 128 : (t + 1) * 128].astype(
            BF16
        )


def block_kernel(
    places,
    where_ref,
    sender_hbm,
    receiver_hbm,
    latent_ref,
    near_ref,
    far_ref,
    cross_ref,
    first_ref,
    second_ref,
    base_ref,
    w_send,
    edge_out,
    edge_hbm,
    edge_t_hbm,
    w_recv_hbm,
    node_in_hbm,
    node_out_hbm,
    node_cot_hbm,
    edge_cot_hbm,
    node_new_hbm,
    edge_new_hbm,
    pre_grad_hbm,
    agg_parts_hbm,
    local_ref,
    keep_upper_ref,
    keep_lower_ref,
    send_upper_ref,
    send_lower_ref,
    own_ref,
    opposite_ref,
    back_first_ref,
    back_second_ref,
    sender,
    receiver,
    table,
    edge_lat,
    edge_t,
    picked,
    w_recv,
    node_x,
    node_in,
    node_out,
    node_cot,
    edge_cot,
    node_new,
    node_act,
    node_lin_grad,
    node_pre_grad,
    agg_parts,
    node_work,
    node_slope,
    edge_new,
    act,
    lin_grad,
    pre_grad,
    work,
    slope,
    normed,
    inverse,
    edge_up,
    back_work,
    weights,
    sums,
    core_sums,
    in_sems,
    out_sems,
):
    feat = edge_out.shape[0]
    nodes = node_cot.shape[0]
    edges = edge_lat.shape[0]
    halo = first_ref.shape[0]
    tiles, _, width = weights.shape
    core = where_ref[0]
    tile = where_ref[1]
    turn = pl.multiple_of(where_ref[2], halo)
    part = tiles * nodes
    held = part + 2 * halo
    loads = Copies(in_sems)
    stores = Copies(out_sems)

    def rows_of(mask):
        return pl.ds(pl.multiple_of((tile ^ mask) * nodes, nodes), nodes)

    first = [
        loads.start(sender_hbm, sender),
        loads.start(receiver_hbm, receiver),
    ]
    second = [loads.start(edge_hbm, edge_lat)]
    third = [
        loads.start(node_in_hbm, node_in),
        loads.start(node_out_hbm, node_out),
        loads.start(node_cot_hbm, node_cot),
    ]
    fourth = [loads.start(edge_cot_hbm, edge_cot)]
    fifth = [
        loads.start(edge_t_hbm, edge_t),
        loads.start(w_recv_hbm.at[2 * feat : 3 * feat], w_recv),
    ]

    for mask, ref in enumerate((latent_ref, near_ref, far_ref, cross_ref)):
        table[rows_of(mask), :] = ref[...]
    table[pl.ds(part + turn, halo), :] = first_ref[...]
    table[pl.ds(part + halo - turn, halo), :] = second_ref[...]
    table[held:, :] = jnp.zeros((table.shape[0] - held, feat), BF16)
    for copy in first:
        copy.wait()
    latent = latent_ref[...]
    node_x[:, 0:feat] = latent
    sender_column = as_column(sender[...])
    receiver_hot = hot_rows(as_column(receiver[...]), nodes)
    receiver_rows = hot_columns(receiver[...], nodes)
    blocks = [slice(at, at + ROWS) for at in range(0, edges, ROWS)]

    def chunks(rows):
        return [slice(at, at + CHUNK) for at in range(rows.start, rows.stop, CHUNK)]

    for rows in blocks:
        hot = hot_rows(sender_column[rows], table.shape[0])
        picked[rows, :] = flat_dot(hot, table[...]).astype(BF16)
    for rows in blocks:
        work[rows, :] = flat_dot(picked[rows, :], w_send[...])
        for c in chunks(rows):
            value, slope[c, :] = silu_pair(base_ref[c, :] + work[c, :])
            act[c, :] = value.astype(BF16)
        normed[rows, :] = flat_dot(act[rows, :], edge_out[...])
        if rows.start == 0:
            for copy in second:
                copy.wait()
        for c in chunks(rows):
            value, scale = layer_norm(normed[c, :])
            normed[c, :] = value
            inverse[c, :] = scale
            edge_new[c, :] = (edge_lat[c, :].astype(F32) + value).astype(BF16)
    stores.start(edge_new, edge_new_hbm)
    node_x[:, feat:] = flat_dot(receiver_rows, edge_new[...]).astype(BF16)

    for copy in third:
        copy.wait()
    node_rows = slice(0, nodes)
    node_work[...] = flat_dot(node_x[...], node_in[...])
    for c in chunks(node_rows):
        value, node_slope[c, :] = silu_pair(node_work[c, :])
        node_act[c, :] = value.astype(BF16)
    node_work[...] = flat_dot(node_act[...], node_out[...])
    for c in chunks(node_rows):
        value, scale = layer_norm(node_work[c, :])
        node_new[c, :] = (node_x[c, 0:feat].astype(F32) + value).astype(BF16)
        up = node_cot[c, :].astype(F32)
        node_lin_grad[c, :] = norm_grad(value, scale, up).astype(BF16)
    stores.start(node_new, node_new_hbm)
    node_work[...] = outer_dot(node_lin_grad[...], node_out[...])
    for c in chunks(node_rows):
        node_pre_grad[c, :] = (node_work[c, :] * node_slope[c, :]).astype(BF16)
    node_work[...] = outer_dot(node_pre_grad[...], node_in[feat:, :])
    for c in chunks(node_rows):
        agg_parts[c, :], low_part = split_parts(node_work[c, :])
        agg_parts[slice(c.start + nodes, c.stop + nodes), :] = low_part
    stores.start(agg_parts, agg_parts_hbm)

    for copy in fourth:
        copy.wait()
    for rows in blocks:
        hot = receiver_hot[rows]
        edge_up[rows, :] = flat_dot(jnp.concatenate([hot, hot], 1), agg_parts[...])
        for c in chunks(rows):
            up = edge_cot[c, :].astype(F32) + edge_up[c, :]
            edge_up[c, :] = up
            lin_grad[c, :] = norm_grad(normed[c, :], inverse[c, :], up).astype(BF16)
        back_work[rows, :] = outer_dot(lin_grad[rows, :], edge_out[...])
        for c in chunks(rows):
            pre_grad[c, :] = (back_work[c, :] * slope[c, :]).astype(BF16)
    stores.start(pre_grad, pre_grad_hbm)
    taken = flat_dot(receiver_rows, pre_grad[...])

    def give(which, keep_ref, send_ref):
        order, low = places[which]
        half = keep_ref.shape[0] // (tiles // 2)
        if order is None:
            for upper in range(tiles // 2):
                to = pl.ds(upper * half, half)
                rows = slice(low, low + half)
                stores.start(weights.at[2 * upper + core, rows], keep_ref.at[to])
                stores.start(weights.at[2 * upper + 1 - core, rows], send_ref.at[to])
            return
        here = {"tile": tile, "dom": where_ref[3]}
        rows = keep_ref.shape[0] >> len(order)
        for index in range(1 << len(order)):
            upper = block = 0
            for at, (axis, bit) in enumerate(order):
                flipped = 1 - ((index >> (len(order) - 1 - at)) & 1)
                value = ((here[axis] >> bit) & 1) ^ flipped
                if axis == "tile":
                    upper = upper + (value << (bit - 1))
                else:
                    block = block + (value << bit)
            source = pl.ds(pl.multiple_of(low + block * rows, 16), rows)
            to = pl.ds(index * rows, rows)
            stores.start(weights.at[2 * upper + core, source], keep_ref.at[to])
            stores.start(weights.at[2 * upper + 1 - core, source], send_ref.at[to])

    part_rows = sums.shape[0] // 2
    for start in (0, part_rows):
        sums[start : start + part_rows, :] = flat_dot(
            hot_columns(sender[...], part_rows, start), pre_grad[...]
        )
    back_first_ref[...] = sums[pl.ds(part + turn, halo), :].astype(BF16)
    back_second_ref[...] = sums[pl.ds(part + halo - turn, halo), :].astype(BF16)
    for mask, ref, first in (
        (0, own_ref, 0),
        (2, opposite_ref, 0),
        (1, core_sums, 0),
        (3, core_sums, part),
    ):
        value = sums[rows_of(mask), :].astype(ref.dtype)
        for at in range(tiles):
            lanes = slice(at * width, (at + 1) * width)
            ref[first + at * nodes : first + (at + 1) * nodes, :] = value[:, lanes]
    stores.start(core_sums, send_upper_ref.at[pl.ds(send_lower_ref.shape[0], 2 * part)])
    put(weights, 4 * feat, inner_dot(node_x[...], node_pre_grad[...]))
    put(weights, 6 * feat, inner_dot(node_act[...], node_lin_grad[...]))
    put(weights, 3 * feat, inner_dot(act[...], lin_grad[...]))
    give(0, keep_upper_ref, send_upper_ref)
    high_part, low_part = split_parts(taken)
    put(weights, 2 * feat, inner_dot(latent, high_part) + inner_dot(latent, low_part))
    put(weights, feat, inner_dot(picked[...], pre_grad[...]))
    for copy in fifth:
        copy.wait()
    put(weights, 0, flat_dot(edge_t[...], pre_grad[...]))
    give(1, keep_lower_ref, send_lower_ref)
    local_ref[...] = (
        node_cot[...].astype(F32)
        + outer_dot(node_pre_grad[...], node_in[0:feat, :])
        + (outer_dot(high_part, w_recv[...]) + outer_dot(low_part, w_recv[...]))
    )
    stores.finish()


def edge_grad_kernel(
    receiver_hbm,
    pre_grad_hbm,
    edge_cot_hbm,
    w_hbm,
    agg_parts_hbm,
    out_hbm,
    receiver,
    pre_grad,
    edge_cot,
    w_edge,
    agg_parts,
    work,
    out,
    in_sems,
    out_sems,
):
    loads, stores = Copies(in_sems), Copies(out_sems)
    for source, target in (
        (receiver_hbm, receiver),
        (agg_parts_hbm, agg_parts),
        (w_hbm.at[0 : w_edge.shape[0]], w_edge),
        (pre_grad_hbm, pre_grad),
        (edge_cot_hbm, edge_cot),
    ):
        loads.start(source, target)
    loads.finish()
    column = as_column(receiver[...])
    for at in range(0, out.shape[0], ROWS):
        rows = slice(at, at + ROWS)
        hot = hot_rows(column[rows], agg_parts.shape[0] // 2)
        work[rows, :] = flat_dot(jnp.concatenate([hot, hot], 1), agg_parts[...]) + outer_dot(
            pre_grad[rows, :], w_edge[...]
        )
        for start in range(at, at + ROWS, CHUNK):
            c = slice(start, start + CHUNK)
            out[c, :] = (edge_cot[c, :].astype(F32) + work[c, :]).astype(BF16)
        stores.start(out.at[rows], out_hbm.at[rows])
    stores.finish()


def node_kernel(
    where_ref,
    from_ref,
    cut_ref,
    w_send_ref,
    local_ref,
    total_ref,
    first_ref,
    second_ref,
    stay_ref,
    slot_ref,
    ends,
):
    nodes, feat = local_ref.shape
    halo = first_ref.shape[0]
    width = total_ref.shape[1]
    turn = pl.multiple_of(where_ref[2], halo)
    ends[pl.ds(turn, halo), :] = first_ref[...]
    ends[pl.ds(halo - turn, halo), :] = second_ref[...]
    value = jnp.concatenate(
        [total_ref[block * nodes : (block + 1) * nodes, :] for block in range(feat // width)], 1
    )
    value = value + flat_dot(hot_columns(cut_ref[...], nodes), ends[...])
    high_part, low_part = split_parts(value)
    w_send = w_send_ref[...]
    grad = local_ref[...] + (outer_dot(high_part, w_send) + outer_dot(low_part, w_send))
    grad = grad.astype(BF16)
    where = from_ref[...]
    slot_ref[...] = flat_dot(hot_columns(where, slot_ref.shape[0], nodes), grad).astype(BF16)
    stay_ref[...] = flat_dot(hot_columns(where, nodes), grad).astype(BF16)


def back_kernel(pick_ref, stay_ref, came_ref, out_hbm, out, out_sems):
    stores = Copies(out_sems)
    hot = hot_columns(pick_ref[...], stay_ref.shape[0])
    out[...] = (stay_ref[...].astype(F32) + flat_dot(hot, came_ref[...])).astype(BF16)
    stores.start(out, out_hbm)
    stores.finish()


def flip(values, axis, mask):
    count = lax.axis_size(axis)
    return lax.ppermute(values, axis, [(i, i ^ mask) for i in range(count)])


def meet(values, axis, step):
    count = lax.axis_size(axis)
    pairs = [(i, (i + (step if i % 2 == 0 else -step)) % count) for i in range(count)]
    return lax.ppermute(values, axis, pairs)


def axis_bits(axis):
    return [(axis, b) for b in range(lax.axis_size(axis).bit_length() - 1)]


def exchange_orders():
    cross, dom_bits = axis_bits("tile")[1:], axis_bits("dom")
    side, line = dom_bits[:1], dom_bits[1:-1]
    return side + cross + line, line + side + cross


def after(values, *others):
    return lax.optimization_barrier((values, others))[0]


def total_of(values):
    return functools.reduce(jnp.add, [v.astype(F32) for v in values])


class Exchange:
    def __init__(self, values, count, order, relative):
        self.values = values
        self.count = count
        self.order = list(order)
        self.relative = relative
        self.outgoing = None

    def cut(self, *others):
        arrays = after(self.values, *others)
        self.count //= 2
        axis, bit = self.order[0]
        mine = (lax.axis_index(axis) >> bit) & 1

        def half(second):
            if self.relative:
                first = int(second) * self.count
                return total_of([a[first : first + self.count] for a in arrays]).astype(BF16)
            first = (mine if second else 1 - mine) * self.count
            return total_of(
                [lax.dynamic_slice_in_dim(a, first, self.count, 0) for a in arrays]
            ).astype(BF16)

        self.outgoing = half(False)
        self.values = [half(True)]
        return self.outgoing

    def send(self):
        axis, bit = self.order.pop(0)
        self.values.append(flip(self.outgoing, axis, 1 << bit))

    def total(self):
        return total_of(self.values)


def cut_all(parts, *others):
    return [part.cut(*others) for part in parts]


def send_all(parts):
    for part in parts:
        part.send()


def body(
    tile_latent,
    relay_pick,
    relay_from,
    cut_pick,
    edge_latent,
    edge_sender,
    edge_receiver,
    edge_in,
    edge_out,
    node_in,
    node_out,
    node_cot,
    edge_cot,
):
    nodes, feat = tile_latent.shape
    edges = edge_latent.shape[0]
    doms, tiles = lax.axis_size("dom"), lax.axis_size("tile")
    slots = relay_pick.shape[1]
    halo = cut_pick.shape[1] // 2
    table_rows = -(-(tiles * nodes + 2 * halo) // nodes) * nodes
    half, width = 7 * feat // 2, feat // tiles
    sds = jax.ShapeDtypeStruct
    node_bf16 = sds((nodes, feat), BF16)
    node_f32 = sds((nodes, feat), F32)
    edge_bf16 = sds((edges, feat), BF16)
    edge_f32 = sds((edges, feat), F32)
    slot_bf16 = sds((slots, feat), BF16)
    halo_bf16 = sds((halo, feat), BF16)
    square = sds((feat, feat), BF16)
    node_index = sds((nodes,), jnp.int32)
    edge_index = sds((edges,), jnp.int32)

    def exchange(rows):
        blocks = rows.reshape(doms, slots // doms, feat)
        return lax.all_to_all(blocks, "dom", split_axis=0, concat_axis=0, tiled=True).reshape(
            slots, feat
        )

    tile = lax.axis_index("tile")
    turn = jnp.where(lax.axis_index("dom") % 2 == 0, halo, 0)
    where = jnp.stack([tile & 1, tile, turn, lax.axis_index("dom")]).astype(jnp.int32)
    outgoing, pick_row = call(
        pick_kernel,
        "pick",
        [Kept(slot_bf16), Kept(relay_pick)],
        [relay_pick, tile_latent],
        [relay_pick, tile_latent, 2],
        limit=SMALL_LIMIT,
    )
    edge_t = jnp.transpose(after(edge_latent, outgoing))
    came = after(exchange(outgoing), edge_t)
    latent, first, second, from_row, cut_row = call(
        pool_kernel,
        "pool",
        [Kept(node_bf16), Kept(halo_bf16), Kept(halo_bf16)]
        + [Kept(sds((1, nodes), jnp.int32)), Kept(cut_pick)],
        [relay_from, cut_pick, tile_latent, Kept(came)],
        [node_index, cut_pick, node_bf16, sds((2 * halo, feat), BF16), 3],
        [where],
        SMALL_LIMIT,
    )
    far = flip(latent, "tile", 2)
    near = flip(latent, "tile", 1)
    first = meet(first, "dom", 1)
    second = meet(second, "dom", -1)
    base, w_send, w_out = call(
        base_kernel,
        "base",
        [Kept(edge_f32), Kept(square), Kept(square)],
        [edge_receiver, edge_latent, edge_in, edge_out, Kept(latent)],
        [edge_index, edge_bf16, square, square, 6],
    )
    across = flip(after(far, first, second, base), "tile", 1)

    orders = exchange_orders()
    rows = 7 * feat // doms
    bits = len(orders[0])
    fine = rows % 16 == 0
    span = tiles * half // 2
    places = [(order if fine else None, low) for order, low in zip(orders, (half, 0))]
    copies = 2 * sum(1 << len(order) if fine else tiles // 2 for order in orders)
    sum_rows = tiles * nodes
    (
        node_new,
        edge_new,
        pre_grad,
        agg_parts,
        local,
        keep_upper,
        keep_lower,
        send_upper,
        send_lower,
        own,
        opposite,
        back_first,
        back_second,
    ) = call(
        functools.partial(block_kernel, places),
        "block",
        [node_bf16, edge_bf16, edge_bf16, sds((2 * nodes, feat), BF16), Kept(node_f32)]
        + [sds((span, width), BF16)] * 2
        + [sds((span + 2 * sum_rows, width), BF16), sds((span, width), BF16)]
        + [Kept(sds((sum_rows, width), F32)), Kept(sds((sum_rows, width), BF16))]
        + [Kept(halo_bf16)] * 2,
        [edge_sender, edge_receiver]
        + [Kept(array) for array in (latent, near, far, across, first, second)]
        + [Kept(base), Kept(w_send), Kept(w_out)]
        + [edge_latent, edge_t, edge_in, node_in, node_out, node_cot, edge_cot],
        [edge_index, edge_index, sds((table_rows, feat), BF16), edge_bf16]
        + [sds((feat, edges), BF16), edge_bf16, square, sds((nodes, 2 * feat), BF16)]
        + [node_in, node_out, node_cot, edge_cot]
        + [node_bf16] * 4
        + [sds((2 * nodes, feat), BF16), node_f32, node_f32]
        + [edge_bf16] * 4
        + [edge_f32] * 3
        + [sds((edges, 1), F32), edge_f32, edge_f32]
        + [sds((tiles, 2 * half, width), BF16), sds((table_rows, feat), F32)]
        + [sds((2 * sum_rows, width), BF16)]
        + [9, 5 + copies],
        [where],
    )
    got_upper = flip(send_upper, "tile", 1)
    got_lower = flip(send_lower, "tile", 1)
    back_first = meet(back_first, "dom", 1)
    back_second = meet(back_second, "dom", -1)
    leaving = (opposite.astype(F32) + got_upper[span + sum_rows :].astype(F32)).astype(BF16)
    across = flip(leaving, "tile", 2)
    parts = []
    for order, keep, got in zip(
        orders, (keep_upper, keep_lower), (got_upper, got_lower), strict=True
    ):
        if fine:
            parts.append(Exchange([keep, got], span, order, True))
            continue
        labels = axis_bits("tile")[:0:-1] + axis_bits("dom")[-2::-1]
        axes = [labels.index(label) for label in order] + [bits, bits + 1]
        values = [
            jnp.transpose(whole.reshape([2] * bits + [rows, width]), axes)
            for whole in (keep, got[:span])
        ]
        parts.append(Exchange([v.reshape(span, width) for v in values], span, order, False))
    sent = parts[0].cut()
    parts[0].send()
    sent = parts[1].cut(sent, back_first, back_second)
    parts[1].send()
    total = own + got_upper[span : span + sum_rows].astype(F32) + across.astype(F32)
    stay, slot_grad = call(
        node_kernel,
        "node",
        [Kept(node_bf16), Kept(slot_bf16)],
        [Kept(array) for array in (from_row, cut_row, w_send, after(local, sent), total)]
        + [Kept(back_first), Kept(back_second)],
        [sds((2 * halo, feat), BF16)],
        [where],
        SMALL_LIMIT,
    )
    back_rows = exchange(slot_grad)
    sent = cut_all(parts, slot_grad)
    send_all(parts)
    [latent_grad] = call(
        back_kernel,
        "back",
        [node_bf16],
        [Kept(pick_row), Kept(stay), Kept(after(back_rows, *sent))],
        [node_bf16, 1],
        limit=SMALL_LIMIT,
    )
    [edge_grad] = call(
        edge_grad_kernel,
        "edge_grad",
        [edge_bf16],
        [edge_receiver, after(pre_grad, latent_grad), edge_cot, edge_in, agg_parts],
        [edge_index, edge_bf16, edge_bf16, square, sds((2 * nodes, feat), BF16)]
        + [edge_f32, edge_bf16, 5, edges // ROWS],
        limit=2 * SMALL_LIMIT,
    )
    first = edge_grad
    while parts[0].order:
        cut_all(parts, first)
        send_all(parts)
        first = ()
    top = axis_bits("dom")[-1][1]
    upper = (lax.axis_index("dom") >> top) & 1
    above, below = [part.total() for part in parts]
    sent = jnp.where(upper == 1, below, above).astype(BF16)
    kept = jnp.where(upper == 1, above, below)
    weight_shard = kept + flip(sent, "dom", 1 << top).astype(F32)
    return (node_new, edge_new, latent_grad, edge_grad, weight_shard)


def solution(mesh):
    rows = P(("dom", "tile"), None)
    flat = P(("dom", "tile"))
    in_specs = (rows, rows, flat, rows, rows, flat, flat, P(), P(), P(), P(), rows, rows)
    out_specs = (rows, rows, rows, rows, P("dom", "tile"))
    return jax.shard_map(body, mesh=mesh, in_specs=in_specs, out_specs=out_specs, check_vma=False)
```

```python
import functools

import jax
import jax.numpy as jnp
from jax import lax
from jax.experimental import pallas as pl
from jax.experimental.pallas import tpu as pltpu
from jax.sharding import PartitionSpec as P

EPSILON = 1e-05
BF16 = jnp.bfloat16
F32 = jnp.float32
ROWS = 256
CHUNK = 32
VMEM_LIMIT = 30 * 1024 * 1024
SMALL_LIMIT = 8 * 1024 * 1024


def layer_norm(values):
    center = values - jnp.mean(values, -1, keepdims=True)
    inverse = lax.rsqrt(jnp.mean(center * center, -1, keepdims=True) + EPSILON)
    return (center * inverse, inverse)


def norm_grad(normed, inverse, upstream):
    mean_up = jnp.mean(upstream, -1, keepdims=True)
    mean_cross = jnp.mean(upstream * normed, -1, keepdims=True)
    return inverse * (upstream - mean_up - normed * mean_cross)


def silu_pair(values):
    sigmoid = 0.5 * jnp.tanh(0.5 * values) + 0.5
    return values * sigmoid, sigmoid * (1.0 + values * (1.0 - sigmoid))


def flat_dot(left_mat, right_mat):
    return jnp.dot(left_mat, right_mat, preferred_element_type=F32)


def inner_dot(left_mat, right_mat):
    return lax.dot_general(
        left_mat, right_mat, (((0,), (0,)), ((), ())), preferred_element_type=F32
    )


def outer_dot(left_mat, right_mat):
    return lax.dot_general(
        left_mat, right_mat, (((1,), (1,)), ((), ())), preferred_element_type=F32
    )


def split_parts(values):
    high_part = values.astype(BF16)
    return high_part, (values - high_part.astype(F32)).astype(BF16)


def marks(hits):
    return jnp.where(hits, 1.0, 0.0).astype(BF16)


def hot_columns(index_row, count, first=0):
    shape = (count, index_row.shape[-1])
    at = lax.broadcasted_iota(jnp.int32, shape, 0) + first
    return marks(jnp.broadcast_to(index_row.reshape(1, -1), shape) == at)


def as_column(index_row):
    shape = (128, index_row.shape[-1])
    return jnp.transpose(jnp.broadcast_to(index_row.reshape(1, -1), shape))


def hot_rows(index_column, count):
    at = lax.broadcasted_iota(jnp.int32, index_column.shape, 1)
    return jnp.concatenate(
        [marks(index_column == at + 128 * k) for k in range(count // 128)], 1
    )


class Kept:
    def __init__(self, array):
        self.array = array


def call(kernel, name, outs, ins, scratch, scalars=(), limit=VMEM_LIMIT):
    def spec(array):
        return pl.BlockSpec(memory_space=pltpu.VMEM if isinstance(array, Kept) else pltpu.HBM)

    def placed(array):
        if isinstance(array, Kept):
            return array.array
        return pltpu.with_memory_space_constraint(array, pltpu.HBM)

    shapes = [
        pltpu.SemaphoreType.DMA((s,)) if isinstance(s, int) else pltpu.VMEM(s.shape, s.dtype)
        for s in scratch
    ]
    return pl.pallas_call(
        kernel,
        out_shape=[
            array.array if isinstance(array, Kept) else pltpu.HBM(array.shape, array.dtype)
            for array in outs
        ],
        in_specs=[pl.BlockSpec(memory_space=pltpu.SMEM)] * len(scalars) + [spec(a) for a in ins],
        out_specs=[spec(array) for array in outs],
        scratch_shapes=shapes,
        compiler_params=pltpu.CompilerParams(vmem_limit_bytes=limit),
        name=name,
    )(*scalars, *[placed(array) for array in ins])


class Copies:
    def __init__(self, sems):
        self.sems = sems
        self.made = 0
        self.open = []

    def start(self, source, target):
        copy = pltpu.make_async_copy(source, target, self.sems.at[self.made])
        copy.start()
        self.made += 1
        self.open.append(copy)
        return copy

    def finish(self):
        for copy in self.open:
            copy.wait()


def pick_kernel(pick_hbm, tile_hbm, out_ref, pick_ref, pick, tile, in_sems):
    loads = Copies(in_sems)
    loads.start(pick_hbm, pick)
    loads.start(tile_hbm, tile)
    loads.finish()
    pick_ref[...] = pick[...]
    rows = hot_rows(as_column(pick[...]), tile.shape[0])
    out_ref[...] = flat_dot(rows, tile[...]).astype(BF16)


def pool_kernel(
    where_ref,
    from_hbm,
    cut_hbm,
    tile_hbm,
    came_ref,
    latent_ref,
    first_ref,
    second_ref,
    from_ref,
    cut_ref,
    at,
    cut,
    tile,
    ends,
    in_sems,
):
    loads = Copies(in_sems)
    for source, target in ((from_hbm, at), (cut_hbm, cut), (tile_hbm, tile)):
        loads.start(source, target)
    loads.finish()
    from_ref[...] = at[...].reshape(from_ref.shape)
    cut_ref[...] = cut[...]
    nodes = tile.shape[0]
    halo = first_ref.shape[0]
    rows = hot_rows(as_column(at[...]), nodes + came_ref.shape[0])
    value = flat_dot(rows[:, :nodes], tile[...]) + flat_dot(rows[:, nodes:], came_ref[...])
    value = value.astype(BF16)
    latent_ref[...] = value
    ends[...] = inner_dot(hot_columns(cut[...], nodes), value).astype(BF16)
    turn = pl.multiple_of(where_ref[2], halo)
    first_ref[...] = ends[pl.ds(turn, halo), :]
    second_ref[...] = ends[pl.ds(halo - turn, halo), :]


def base_kernel(
    receiver_hbm,
    edge_hbm,
    edge_in_hbm,
    edge_out_hbm,
    latent_ref,
    base_ref,
    w_send_ref,
    edge_out_ref,
    receiver,
    edge_lat,
    w_edge,
    w_recv,
    in_sems,
):
    feat = edge_out_ref.shape[0]
    loads = Copies(in_sems)
    first = [
        loads.start(receiver_hbm, receiver),
        loads.start(edge_hbm, edge_lat),
        loads.start(edge_in_hbm.at[0:feat], w_edge),
        loads.start(edge_in_hbm.at[2 * feat : 3 * feat], w_recv),
    ]
    second = [
        loads.start(edge_in_hbm.at[feat : 2 * feat], w_send_ref),
        loads.start(edge_out_hbm, edge_out_ref),
    ]
    for copy in first:
        copy.wait()
    column = as_column(receiver[...])
    latent = latent_ref[...]
    for at in range(0, edge_lat.shape[0], ROWS):
        rows = slice(at, at + ROWS)
        taken = flat_dot(hot_rows(column[rows], latent.shape[0]), latent).astype(BF16)
        base_ref[rows, :] = flat_dot(edge_lat[rows, :], w_edge[...]) + flat_dot(taken, w_recv[...])
    for copy in second:
        copy.wait()


def put(weights, first, terms):
    for t in range(terms.shape[1] // 128):
        weights[t, first : first + terms.shape[0], :] = terms[:, t * 128 : (t + 1) * 128].astype(
            BF16
        )


def block_kernel(
    places,
    where_ref,
    sender_hbm,
    receiver_hbm,
    latent_ref,
    near_ref,
    far_ref,
    cross_ref,
    first_ref,
    second_ref,
    base_ref,
    w_send,
    edge_out,
    edge_hbm,
    edge_t_hbm,
    w_recv_hbm,
    node_in_hbm,
    node_out_hbm,
    node_cot_hbm,
    edge_cot_hbm,
    node_new_hbm,
    edge_new_hbm,
    pre_grad_hbm,
    agg_parts_hbm,
    local_ref,
    keep_upper_ref,
    keep_lower_ref,
    send_upper_ref,
    send_lower_ref,
    own_ref,
    opposite_ref,
    back_first_ref,
    back_second_ref,
    sender,
    receiver,
    table,
    edge_lat,
    edge_t,
    picked,
    w_recv,
    node_x,
    node_in,
    node_out,
    node_cot,
    edge_cot,
    node_new,
    node_act,
    node_lin_grad,
    node_pre_grad,
    agg_parts,
    node_work,
    node_slope,
    edge_new,
    act,
    lin_grad,
    pre_grad,
    work,
    slope,
    normed,
    inverse,
    edge_up,
    back_work,
    weights,
    sums,
    core_sums,
    in_sems,
    out_sems,
):
    feat = edge_out.shape[0]
    nodes = node_cot.shape[0]
    edges = edge_lat.shape[0]
    halo = first_ref.shape[0]
    tiles, _, width = weights.shape
    core = where_ref[0]
    tile = where_ref[1]
    turn = pl.multiple_of(where_ref[2], halo)
    part = tiles * nodes
    held = part + 2 * halo
    loads = Copies(in_sems)
    stores = Copies(out_sems)

    def rows_of(mask):
        return pl.ds(pl.multiple_of((tile ^ mask) * nodes, nodes), nodes)

    first = [
        loads.start(sender_hbm, sender),
        loads.start(receiver_hbm, receiver),
    ]
    second = [loads.start(edge_hbm, edge_lat)]
    third = [
        loads.start(node_in_hbm, node_in),
        loads.start(node_out_hbm, node_out),
        loads.start(node_cot_hbm, node_cot),
    ]
    fourth = [loads.start(edge_cot_hbm, edge_cot)]
    fifth = [
        loads.start(edge_t_hbm, edge_t),
        loads.start(w_recv_hbm.at[2 * feat : 3 * feat], w_recv),
    ]

    for mask, ref in enumerate((latent_ref, near_ref, far_ref, cross_ref)):
        table[rows_of(mask), :] = ref[...]
    table[pl.ds(part + turn, halo), :] = first_ref[...]
    table[pl.ds(part + halo - turn, halo), :] = second_ref[...]
    table[held:, :] = jnp.zeros((table.shape[0] - held, feat), BF16)
    for copy in first:
        copy.wait()
    latent = latent_ref[...]
    node_x[:, 0:feat] = latent
    sender_column = as_column(sender[...])
    receiver_hot = hot_rows(as_column(receiver[...]), nodes)
    receiver_rows = hot_columns(receiver[...], nodes)
    blocks = [slice(at, at + ROWS) for at in range(0, edges, ROWS)]

    def chunks(rows):
        return [slice(at, at + CHUNK) for at in range(rows.start, rows.stop, CHUNK)]

    for rows in blocks:
        hot = hot_rows(sender_column[rows], table.shape[0])
        picked[rows, :] = flat_dot(hot, table[...]).astype(BF16)
    for rows in blocks:
        work[rows, :] = flat_dot(picked[rows, :], w_send[...])
        for c in chunks(rows):
            value, slope[c, :] = silu_pair(base_ref[c, :] + work[c, :])
            act[c, :] = value.astype(BF16)
        normed[rows, :] = flat_dot(act[rows, :], edge_out[...])
        if rows.start == 0:
            for copy in second:
                copy.wait()
        for c in chunks(rows):
            value, scale = layer_norm(normed[c, :])
            normed[c, :] = value
            inverse[c, :] = scale
            edge_new[c, :] = (edge_lat[c, :].astype(F32) + value).astype(BF16)
    stores.start(edge_new, edge_new_hbm)
    node_x[:, feat:] = flat_dot(receiver_rows, edge_new[...]).astype(BF16)

    for copy in third:
        copy.wait()
    node_rows = slice(0, nodes)
    node_work[...] = flat_dot(node_x[...], node_in[...])
    for c in chunks(node_rows):
        value, node_slope[c, :] = silu_pair(node_work[c, :])
        node_act[c, :] = value.astype(BF16)
    node_work[...] = flat_dot(node_act[...], node_out[...])
    for c in chunks(node_rows):
        value, scale = layer_norm(node_work[c, :])
        node_new[c, :] = (node_x[c, 0:feat].astype(F32) + value).astype(BF16)
        up = node_cot[c, :].astype(F32)
        node_lin_grad[c, :] = norm_grad(value, scale, up).astype(BF16)
    stores.start(node_new, node_new_hbm)
    node_work[...] = outer_dot(node_lin_grad[...], node_out[...])
    for c in chunks(node_rows):
        node_pre_grad[c, :] = (node_work[c, :] * node_slope[c, :]).astype(BF16)
    node_work[...] = outer_dot(node_pre_grad[...], node_in[feat:, :])
    for c in chunks(node_rows):
        agg_parts[c, :], low_part = split_parts(node_work[c, :])
        agg_parts[slice(c.start + nodes, c.stop + nodes), :] = low_part
    stores.start(agg_parts, agg_parts_hbm)

    for copy in fourth:
        copy.wait()
    for rows in blocks:
        hot = receiver_hot[rows]
        edge_up[rows, :] = flat_dot(jnp.concatenate([hot, hot], 1), agg_parts[...])
        for c in chunks(rows):
            up = edge_cot[c, :].astype(F32) + edge_up[c, :]
            edge_up[c, :] = up
            lin_grad[c, :] = norm_grad(normed[c, :], inverse[c, :], up).astype(BF16)
        back_work[rows, :] = outer_dot(lin_grad[rows, :], edge_out[...])
        for c in chunks(rows):
            pre_grad[c, :] = (back_work[c, :] * slope[c, :]).astype(BF16)
    stores.start(pre_grad, pre_grad_hbm)
    taken = flat_dot(receiver_rows, pre_grad[...])

    def give(which, keep_ref, send_ref):
        order, low = places[which]
        half = keep_ref.shape[0] // (tiles // 2)
        if order is None:
            for upper in range(tiles // 2):
                to = pl.ds(upper * half, half)
                rows = slice(low, low + half)
                stores.start(weights.at[2 * upper + core, rows], keep_ref.at[to])
                stores.start(weights.at[2 * upper + 1 - core, rows], send_ref.at[to])
            return
        here = {"tile": tile, "dom": where_ref[3]}
        rows = keep_ref.shape[0] >> len(order)
        for index in range(1 << len(order)):
            upper = block = 0
            for at, (axis, bit) in enumerate(order):
                flipped = 1 - ((index >> (len(order) - 1 - at)) & 1)
                value = ((here[axis] >> bit) & 1) ^ flipped
                if axis == "tile":
                    upper = upper + (value << (bit - 1))
                else:
                    block = block + (value << bit)
            source = pl.ds(pl.multiple_of(low + block * rows, 16), rows)
            to = pl.ds(index * rows, rows)
            stores.start(weights.at[2 * upper + core, source], keep_ref.at[to])
            stores.start(weights.at[2 * upper + 1 - core, source], send_ref.at[to])

    part_rows = sums.shape[0] // 2
    for start in (0, part_rows):
        sums[start : start + part_rows, :] = flat_dot(
            hot_columns(sender[...], part_rows, start), pre_grad[...]
        )
    back_first_ref[...] = sums[pl.ds(part + turn, halo), :].astype(BF16)
    back_second_ref[...] = sums[pl.ds(part + halo - turn, halo), :].astype(BF16)
    for mask, ref, first in (
        (0, own_ref, 0),
        (2, opposite_ref, 0),
        (1, core_sums, 0),
        (3, core_sums, part),
    ):
        value = sums[rows_of(mask), :].astype(ref.dtype)
        for at in range(tiles):
            lanes = slice(at * width, (at + 1) * width)
            ref[first + at * nodes : first + (at + 1) * nodes, :] = value[:, lanes]
    stores.start(core_sums, send_upper_ref.at[pl.ds(send_lower_ref.shape[0], 2 * part)])
    put(weights, 4 * feat, inner_dot(node_x[...], node_pre_grad[...]))
    put(weights, 6 * feat, inner_dot(node_act[...], node_lin_grad[...]))
    put(weights, 3 * feat, inner_dot(act[...], lin_grad[...]))
    give(0, keep_upper_ref, send_upper_ref)
    high_part, low_part = split_parts(taken)
    put(weights, 2 * feat, inner_dot(latent, high_part) + inner_dot(latent, low_part))
    put(weights, feat, inner_dot(picked[...], pre_grad[...]))
    for copy in fifth:
        copy.wait()
    put(weights, 0, flat_dot(edge_t[...], pre_grad[...]))
    give(1, keep_lower_ref, send_lower_ref)
    local_ref[...] = (
        node_cot[...].astype(F32)
        + outer_dot(node_pre_grad[...], node_in[0:feat, :])
        + (outer_dot(high_part, w_recv[...]) + outer_dot(low_part, w_recv[...]))
    )
    stores.finish()


def edge_grad_kernel(
    receiver_hbm,
    pre_grad_hbm,
    edge_cot_hbm,
    w_hbm,
    agg_parts_hbm,
    out_hbm,
    receiver,
    pre_grad,
    edge_cot,
    w_edge,
    agg_parts,
    work,
    out,
    in_sems,
    out_sems,
):
    loads, stores = Copies(in_sems), Copies(out_sems)
    for source, target in (
        (receiver_hbm, receiver),
        (agg_parts_hbm, agg_parts),
        (w_hbm.at[0 : w_edge.shape[0]], w_edge),
        (pre_grad_hbm, pre_grad),
        (edge_cot_hbm, edge_cot),
    ):
        loads.start(source, target)
    loads.finish()
    column = as_column(receiver[...])
    for at in range(0, out.shape[0], ROWS):
        rows = slice(at, at + ROWS)
        hot = hot_rows(column[rows], agg_parts.shape[0] // 2)
        work[rows, :] = flat_dot(jnp.concatenate([hot, hot], 1), agg_parts[...]) + outer_dot(
            pre_grad[rows, :], w_edge[...]
        )
        for start in range(at, at + ROWS, CHUNK):
            c = slice(start, start + CHUNK)
            out[c, :] = (edge_cot[c, :].astype(F32) + work[c, :]).astype(BF16)
        stores.start(out.at[rows], out_hbm.at[rows])
    stores.finish()


def node_kernel(
    where_ref,
    from_ref,
    cut_ref,
    w_send_ref,
    local_ref,
    total_ref,
    first_ref,
    second_ref,
    stay_ref,
    slot_ref,
    ends,
):
    nodes, feat = local_ref.shape
    halo = first_ref.shape[0]
    width = total_ref.shape[1]
    turn = pl.multiple_of(where_ref[2], halo)
    ends[pl.ds(turn, halo), :] = first_ref[...]
    ends[pl.ds(halo - turn, halo), :] = second_ref[...]
    value = jnp.concatenate(
        [total_ref[block * nodes : (block + 1) * nodes, :] for block in range(feat // width)], 1
    )
    value = value + flat_dot(hot_columns(cut_ref[...], nodes), ends[...])
    high_part, low_part = split_parts(value)
    w_send = w_send_ref[...]
    grad = local_ref[...] + (outer_dot(high_part, w_send) + outer_dot(low_part, w_send))
    grad = grad.astype(BF16)
    where = from_ref[...]
    slot_ref[...] = flat_dot(hot_columns(where, slot_ref.shape[0], nodes), grad).astype(BF16)
    stay_ref[...] = flat_dot(hot_columns(where, nodes), grad).astype(BF16)


def back_kernel(pick_ref, stay_ref, came_ref, out_hbm, out, out_sems):
    stores = Copies(out_sems)
    hot = hot_columns(pick_ref[...], stay_ref.shape[0])
    out[...] = (stay_ref[...].astype(F32) + flat_dot(hot, came_ref[...])).astype(BF16)
    stores.start(out, out_hbm)
    stores.finish()


def flip(values, axis, mask):
    count = lax.axis_size(axis)
    return lax.ppermute(values, axis, [(i, i ^ mask) for i in range(count)])


def meet(values, axis, step):
    count = lax.axis_size(axis)
    pairs = [(i, (i + (step if i % 2 == 0 else -step)) % count) for i in range(count)]
    return lax.ppermute(values, axis, pairs)


def axis_bits(axis):
    return [(axis, b) for b in range(lax.axis_size(axis).bit_length() - 1)]


def exchange_orders():
    cross, dom_bits = axis_bits("tile")[1:], axis_bits("dom")
    side, line = dom_bits[:1], dom_bits[1:-1]
    return side + cross + line, line + side + cross


def after(values, *others):
    return lax.optimization_barrier((values, others))[0]


def total_of(values):
    return functools.reduce(jnp.add, [v.astype(F32) for v in values])


class Exchange:
    def __init__(self, values, count, order, relative):
        self.values = values
        self.count = count
        self.order = list(order)
        self.relative = relative
        self.outgoing = None

    def cut(self, *others):
        arrays = after(self.values, *others)
        self.count //= 2
        axis, bit = self.order[0]
        mine = (lax.axis_index(axis) >> bit) & 1

        def half(second):
            if self.relative:
                first = int(second) * self.count
                return total_of([a[first : first + self.count] for a in arrays]).astype(BF16)
            first = (mine if second else 1 - mine) * self.count
            return total_of(
                [lax.dynamic_slice_in_dim(a, first, self.count, 0) for a in arrays]
            ).astype(BF16)

        self.outgoing = half(False)
        self.values = [half(True)]
        return self.outgoing

    def send(self):
        axis, bit = self.order.pop(0)
        self.values.append(flip(self.outgoing, axis, 1 << bit))

    def total(self):
        return total_of(self.values)


def cut_all(parts, *others):
    return [part.cut(*others) for part in parts]


def send_all(parts):
    for part in parts:
        part.send()


def body(
    tile_latent,
    relay_pick,
    relay_from,
    cut_pick,
    edge_latent,
    edge_sender,
    edge_receiver,
    edge_in,
    edge_out,
    node_in,
    node_out,
    node_cot,
    edge_cot,
):
    nodes, feat = tile_latent.shape
    edges = edge_latent.shape[0]
    doms, tiles = lax.axis_size("dom"), lax.axis_size("tile")
    slots = relay_pick.shape[1]
    halo = cut_pick.shape[1] // 2
    table_rows = -(-(tiles * nodes + 2 * halo) // nodes) * nodes
    half, width = 7 * feat // 2, feat // tiles
    sds = jax.ShapeDtypeStruct
    node_bf16 = sds((nodes, feat), BF16)
    node_f32 = sds((nodes, feat), F32)
    edge_bf16 = sds((edges, feat), BF16)
    edge_f32 = sds((edges, feat), F32)
    slot_bf16 = sds((slots, feat), BF16)
    halo_bf16 = sds((halo, feat), BF16)
    square = sds((feat, feat), BF16)
    node_index = sds((nodes,), jnp.int32)
    edge_index = sds((edges,), jnp.int32)

    def exchange(rows):
        blocks = rows.reshape(doms, slots // doms, feat)
        return lax.all_to_all(blocks, "dom", split_axis=0, concat_axis=0, tiled=True).reshape(
            slots, feat
        )

    tile = lax.axis_index("tile")
    turn = jnp.where(lax.axis_index("dom") % 2 == 0, halo, 0)
    where = jnp.stack([tile & 1, tile, turn, lax.axis_index("dom")]).astype(jnp.int32)
    outgoing, pick_row = call(
        pick_kernel,
        "pick",
        [Kept(slot_bf16), Kept(relay_pick)],
        [relay_pick, tile_latent],
        [relay_pick, tile_latent, 2],
        limit=SMALL_LIMIT,
    )
    edge_t = jnp.transpose(after(edge_latent, outgoing))
    came = after(exchange(outgoing), edge_t)
    latent, first, second, from_row, cut_row = call(
        pool_kernel,
        "pool",
        [Kept(node_bf16), Kept(halo_bf16), Kept(halo_bf16)]
        + [Kept(sds((1, nodes), jnp.int32)), Kept(cut_pick)],
        [relay_from, cut_pick, tile_latent, Kept(came)],
        [node_index, cut_pick, node_bf16, sds((2 * halo, feat), BF16), 3],
        [where],
        SMALL_LIMIT,
    )
    far = flip(latent, "tile", 2)
    near = flip(latent, "tile", 1)
    first = meet(first, "dom", 1)
    second = meet(second, "dom", -1)
    base, w_send, w_out = call(
        base_kernel,
        "base",
        [Kept(edge_f32), Kept(square), Kept(square)],
        [edge_receiver, edge_latent, edge_in, edge_out, Kept(latent)],
        [edge_index, edge_bf16, square, square, 6],
    )
    across = flip(after(far, first, second, base), "tile", 1)

    orders = exchange_orders()
    rows = 7 * feat // doms
    bits = len(orders[0])
    fine = rows % 16 == 0
    span = tiles * half // 2
    places = [(order if fine else None, low) for order, low in zip(orders, (half, 0))]
    copies = 2 * sum(1 << len(order) if fine else tiles // 2 for order in orders)
    sum_rows = tiles * nodes
    (
        node_new,
        edge_new,
        pre_grad,
        agg_parts,
        local,
        keep_upper,
        keep_lower,
        send_upper,
        send_lower,
        own,
        opposite,
        back_first,
        back_second,
    ) = call(
        functools.partial(block_kernel, places),
        "block",
        [node_bf16, edge_bf16, edge_bf16, sds((2 * nodes, feat), BF16), Kept(node_f32)]
        + [sds((span, width), BF16)] * 2
        + [sds((span + 2 * sum_rows, width), BF16), sds((span, width), BF16)]
        + [Kept(sds((sum_rows, width), F32)), Kept(sds((sum_rows, width), BF16))]
        + [Kept(halo_bf16)] * 2,
        [edge_sender, edge_receiver]
        + [Kept(array) for array in (latent, near, far, across, first, second)]
        + [Kept(base), Kept(w_send), Kept(w_out)]
        + [edge_latent, edge_t, edge_in, node_in, node_out, node_cot, edge_cot],
        [edge_index, edge_index, sds((table_rows, feat), BF16), edge_bf16]
        + [sds((feat, edges), BF16), edge_bf16, square, sds((nodes, 2 * feat), BF16)]
        + [node_in, node_out, node_cot, edge_cot]
        + [node_bf16] * 4
        + [sds((2 * nodes, feat), BF16), node_f32, node_f32]
        + [edge_bf16] * 4
        + [edge_f32] * 3
        + [sds((edges, 1), F32), edge_f32, edge_f32]
        + [sds((tiles, 2 * half, width), BF16), sds((table_rows, feat), F32)]
        + [sds((2 * sum_rows, width), BF16)]
        + [9, 5 + copies],
        [where],
    )
    got_upper = flip(send_upper, "tile", 1)
    got_lower = flip(send_lower, "tile", 1)
    back_first = meet(back_first, "dom", 1)
    back_second = meet(back_second, "dom", -1)
    leaving = (opposite.astype(F32) + got_upper[span + sum_rows :].astype(F32)).astype(BF16)
    across = flip(leaving, "tile", 2)
    parts = []
    for order, keep, got in zip(
        orders, (keep_upper, keep_lower), (got_upper, got_lower), strict=True
    ):
        if fine:
            parts.append(Exchange([keep, got], span, order, True))
            continue
        labels = axis_bits("tile")[:0:-1] + axis_bits("dom")[-2::-1]
        axes = [labels.index(label) for label in order] + [bits, bits + 1]
        values = [
            jnp.transpose(whole.reshape([2] * bits + [rows, width]), axes)
            for whole in (keep, got[:span])
        ]
        parts.append(Exchange([v.reshape(span, width) for v in values], span, order, False))
    sent = parts[0].cut()
    parts[0].send()
    sent = parts[1].cut(sent, back_first, back_second)
    parts[1].send()
    total = own + got_upper[span : span + sum_rows].astype(F32) + across.astype(F32)
    stay, slot_grad = call(
        node_kernel,
        "node",
        [Kept(node_bf16), Kept(slot_bf16)],
        [Kept(array) for array in (from_row, cut_row, w_send, after(local, sent), total)]
        + [Kept(back_first), Kept(back_second)],
        [sds((2 * halo, feat), BF16)],
        [where],
        SMALL_LIMIT,
    )
    back_rows = exchange(slot_grad)
    sent = cut_all(parts, slot_grad)
    send_all(parts)
    [latent_grad] = call(
        back_kernel,
        "back",
        [node_bf16],
        [Kept(pick_row), Kept(stay), Kept(after(back_rows, *sent))],
        [node_bf16, 1],
        limit=SMALL_LIMIT,
    )
    first = latent_grad
    while parts[0].order:
        sent = cut_all(parts, first)
        send_all(parts)
        first = ()
    [edge_grad] = call(
        edge_grad_kernel,
        "edge_grad",
        [edge_bf16],
        [edge_receiver, after(pre_grad, *sent), edge_cot, edge_in, agg_parts],
        [edge_index, edge_bf16, edge_bf16, square, sds((2 * nodes, feat), BF16)]
        + [edge_f32, edge_bf16, 5, edges // ROWS],
        limit=2 * SMALL_LIMIT,
    )
    for part in parts:
        part.values = after(part.values, edge_grad)
    top = axis_bits("dom")[-1][1]
    upper = (lax.axis_index("dom") >> top) & 1
    above, below = [part.total() for part in parts]
    sent = jnp.where(upper == 1, below, above).astype(BF16)
    kept = jnp.where(upper == 1, above, below)
    weight_shard = kept + flip(sent, "dom", 1 << top).astype(F32)
    return (node_new, edge_new, latent_grad, edge_grad, weight_shard)


def solution(mesh):
    rows = P(("dom", "tile"), None)
    flat = P(("dom", "tile"))
    in_specs = (rows, rows, flat, rows, rows, flat, flat, P(), P(), P(), P(), rows, rows)
    out_specs = (rows, rows, rows, rows, P("dom", "tile"))
    return jax.shard_map(body, mesh=mesh, in_specs=in_specs, out_specs=out_specs, check_vma=False)
```

```python
import functools

import jax
import jax.numpy as jnp
from jax import lax
from jax.experimental import pallas as pl
from jax.experimental.pallas import tpu as pltpu
from jax.sharding import PartitionSpec as P

EPSILON = 1e-05
BF16 = jnp.bfloat16
F32 = jnp.float32
ROWS = 384
CHUNK = 32
VMEM_LIMIT = 30 * 1024 * 1024
SMALL_LIMIT = 8 * 1024 * 1024


def layer_norm(values):
    center = values - jnp.mean(values, -1, keepdims=True)
    inverse = lax.rsqrt(jnp.mean(center * center, -1, keepdims=True) + EPSILON)
    return (center * inverse, inverse)


def norm_grad(normed, inverse, upstream):
    mean_up = jnp.mean(upstream, -1, keepdims=True)
    mean_cross = jnp.mean(upstream * normed, -1, keepdims=True)
    return inverse * (upstream - mean_up - normed * mean_cross)


def silu_pair(values):
    sigmoid = 0.5 * jnp.tanh(0.5 * values) + 0.5
    return values * sigmoid, sigmoid * (1.0 + values * (1.0 - sigmoid))


def flat_dot(left_mat, right_mat):
    return jnp.dot(left_mat, right_mat, preferred_element_type=F32)


def inner_dot(left_mat, right_mat):
    return lax.dot_general(
        left_mat, right_mat, (((0,), (0,)), ((), ())), preferred_element_type=F32
    )


def outer_dot(left_mat, right_mat):
    return lax.dot_general(
        left_mat, right_mat, (((1,), (1,)), ((), ())), preferred_element_type=F32
    )


def split_parts(values):
    high_part = values.astype(BF16)
    return high_part, (values - high_part.astype(F32)).astype(BF16)


def marks(hits):
    return jnp.where(hits, 1.0, 0.0).astype(BF16)


def hot_columns(index_row, count, first=0):
    shape = (count, index_row.shape[-1])
    at = lax.broadcasted_iota(jnp.int32, shape, 0) + first
    return marks(jnp.broadcast_to(index_row.reshape(1, -1), shape) == at)


def as_column(index_row):
    shape = (128, index_row.shape[-1])
    return jnp.transpose(jnp.broadcast_to(index_row.reshape(1, -1), shape))


def hot_rows(index_column, count):
    at = lax.broadcasted_iota(jnp.int32, index_column.shape, 1)
    return jnp.concatenate(
        [marks(index_column == at + 128 * k) for k in range(count // 128)], 1
    )


class Kept:
    def __init__(self, array):
        self.array = array


def call(kernel, name, outs, ins, scratch, scalars=(), limit=VMEM_LIMIT):
    def spec(array):
        return pl.BlockSpec(memory_space=pltpu.VMEM if isinstance(array, Kept) else pltpu.HBM)

    def placed(array):
        if isinstance(array, Kept):
            return array.array
        return pltpu.with_memory_space_constraint(array, pltpu.HBM)

    shapes = [
        pltpu.SemaphoreType.DMA((s,)) if isinstance(s, int) else pltpu.VMEM(s.shape, s.dtype)
        for s in scratch
    ]
    return pl.pallas_call(
        kernel,
        out_shape=[
            array.array if isinstance(array, Kept) else pltpu.HBM(array.shape, array.dtype)
            for array in outs
        ],
        in_specs=[pl.BlockSpec(memory_space=pltpu.SMEM)] * len(scalars) + [spec(a) for a in ins],
        out_specs=[spec(array) for array in outs],
        scratch_shapes=shapes,
        compiler_params=pltpu.CompilerParams(vmem_limit_bytes=limit),
        name=name,
    )(*scalars, *[placed(array) for array in ins])


class Copies:
    def __init__(self, sems):
        self.sems = sems
        self.made = 0
        self.open = []

    def start(self, source, target):
        copy = pltpu.make_async_copy(source, target, self.sems.at[self.made])
        copy.start()
        self.made += 1
        self.open.append(copy)
        return copy

    def finish(self):
        for copy in self.open:
            copy.wait()


def pick_kernel(
    pick_hbm,
    tile_hbm,
    from_hbm,
    cut_hbm,
    out_ref,
    pick_ref,
    tile_ref,
    from_ref,
    cut_ref,
    at,
    in_sems,
):
    loads = Copies(in_sems)
    first = [loads.start(pick_hbm, pick_ref), loads.start(tile_hbm, tile_ref)]
    second = [loads.start(from_hbm, at), loads.start(cut_hbm, cut_ref)]
    for copy in first:
        copy.wait()
    rows = hot_rows(as_column(pick_ref[...]), tile_ref.shape[0])
    out_ref[...] = flat_dot(rows, tile_ref[...]).astype(BF16)
    for copy in second:
        copy.wait()
    from_ref[...] = at[...].reshape(from_ref.shape)


def pool_kernel(
    where_ref,
    from_ref,
    cut_ref,
    tile_ref,
    came_ref,
    latent_ref,
    first_ref,
    second_ref,
    ends,
):
    nodes = tile_ref.shape[0]
    halo = first_ref.shape[0]
    rows = hot_rows(as_column(from_ref[...]), nodes + came_ref.shape[0])
    value = flat_dot(rows[:, :nodes], tile_ref[...]) + flat_dot(rows[:, nodes:], came_ref[...])
    value = value.astype(BF16)
    latent_ref[...] = value
    ends[...] = inner_dot(hot_columns(cut_ref[...], nodes), value).astype(BF16)
    turn = pl.multiple_of(where_ref[2], halo)
    first_ref[...] = ends[pl.ds(turn, halo), :]
    second_ref[...] = ends[pl.ds(halo - turn, halo), :]


def base_kernel(
    receiver_hbm,
    edge_hbm,
    edge_in_hbm,
    edge_out_hbm,
    latent_ref,
    base_ref,
    w_send_ref,
    edge_out_ref,
    receiver,
    edge_lat,
    w_edge,
    w_recv,
    in_sems,
):
    feat = edge_out_ref.shape[0]
    loads = Copies(in_sems)
    first = [
        loads.start(receiver_hbm, receiver),
        loads.start(edge_hbm, edge_lat),
        loads.start(edge_in_hbm.at[0:feat], w_edge),
        loads.start(edge_in_hbm.at[2 * feat : 3 * feat], w_recv),
    ]
    second = [
        loads.start(edge_in_hbm.at[feat : 2 * feat], w_send_ref),
        loads.start(edge_out_hbm, edge_out_ref),
    ]
    for copy in first:
        copy.wait()
    column = as_column(receiver[...])
    latent = latent_ref[...]
    for at in range(0, edge_lat.shape[0], ROWS):
        rows = slice(at, at + ROWS)
        taken = flat_dot(hot_rows(column[rows], latent.shape[0]), latent).astype(BF16)
        base_ref[rows, :] = flat_dot(edge_lat[rows, :], w_edge[...]) + flat_dot(taken, w_recv[...])
    for copy in second:
        copy.wait()


def put(weights, first, terms):
    for t in range(terms.shape[1] // 128):
        weights[t, first : first + terms.shape[0], :] = terms[:, t * 128 : (t + 1) * 128].astype(
            BF16
        )


def block_kernel(
    places,
    where_ref,
    sender_hbm,
    receiver_hbm,
    latent_ref,
    near_ref,
    far_ref,
    cross_ref,
    first_ref,
    second_ref,
    base_ref,
    w_send,
    edge_out,
    edge_hbm,
    edge_t_hbm,
    w_recv_hbm,
    node_in_hbm,
    node_out_hbm,
    node_cot_hbm,
    edge_cot_hbm,
    node_new_hbm,
    edge_new_hbm,
    pre_grad_hbm,
    agg_parts_hbm,
    local_ref,
    keep_upper_ref,
    keep_lower_ref,
    send_upper_ref,
    send_lower_ref,
    own_ref,
    opposite_ref,
    back_first_ref,
    back_second_ref,
    sender,
    receiver,
    table,
    edge_lat,
    edge_t,
    picked,
    w_recv,
    node_x,
    node_in,
    node_out,
    node_cot,
    edge_cot,
    node_new,
    node_act,
    node_lin_grad,
    node_pre_grad,
    agg_parts,
    node_work,
    node_slope,
    edge_new,
    act,
    lin_grad,
    pre_grad,
    work,
    slope,
    normed,
    inverse,
    edge_up,
    back_work,
    weights,
    sums,
    core_sums,
    in_sems,
    out_sems,
):
    feat = edge_out.shape[0]
    nodes = node_cot.shape[0]
    edges = edge_lat.shape[0]
    halo = first_ref.shape[0]
    tiles, _, width = weights.shape
    core = where_ref[0]
    tile = where_ref[1]
    turn = pl.multiple_of(where_ref[2], halo)
    part = tiles * nodes
    held = part + 2 * halo
    loads = Copies(in_sems)
    stores = Copies(out_sems)

    def rows_of(mask):
        return pl.ds(pl.multiple_of((tile ^ mask) * nodes, nodes), nodes)

    first = [
        loads.start(sender_hbm, sender),
        loads.start(receiver_hbm, receiver),
    ]
    second = [loads.start(edge_hbm, edge_lat)]
    third = [
        loads.start(node_in_hbm, node_in),
        loads.start(node_out_hbm, node_out),
        loads.start(node_cot_hbm, node_cot),
    ]
    fourth = [loads.start(edge_cot_hbm, edge_cot)]
    fifth = [
        loads.start(edge_t_hbm, edge_t),
        loads.start(w_recv_hbm.at[2 * feat : 3 * feat], w_recv),
    ]

    for mask, ref in enumerate((latent_ref, near_ref, far_ref, cross_ref)):
        table[rows_of(mask), :] = ref[...]
    table[pl.ds(part + turn, halo), :] = first_ref[...]
    table[pl.ds(part + halo - turn, halo), :] = second_ref[...]
    table[held:, :] = jnp.zeros((table.shape[0] - held, feat), BF16)
    for copy in first:
        copy.wait()
    latent = latent_ref[...]
    node_x[:, 0:feat] = latent
    sender_column = as_column(sender[...])
    receiver_hot = hot_rows(as_column(receiver[...]), nodes)
    receiver_rows = hot_columns(receiver[...], nodes)
    blocks = [slice(at, at + ROWS) for at in range(0, edges, ROWS)]

    def chunks(rows):
        return [slice(at, at + CHUNK) for at in range(rows.start, rows.stop, CHUNK)]

    for rows in blocks:
        hot = hot_rows(sender_column[rows], table.shape[0])
        picked[rows, :] = flat_dot(hot, table[...]).astype(BF16)
    for rows in blocks:
        work[rows, :] = flat_dot(picked[rows, :], w_send[...])
        for c in chunks(rows):
            value, slope[c, :] = silu_pair(base_ref[c, :] + work[c, :])
            act[c, :] = value.astype(BF16)
        normed[rows, :] = flat_dot(act[rows, :], edge_out[...])
        if rows.start == 0:
            for copy in second:
                copy.wait()
        for c in chunks(rows):
            value, scale = layer_norm(normed[c, :])
            normed[c, :] = value
            inverse[c, :] = scale
            edge_new[c, :] = (edge_lat[c, :].astype(F32) + value).astype(BF16)
    stores.start(edge_new, edge_new_hbm)
    node_x[:, feat:] = flat_dot(receiver_rows, edge_new[...]).astype(BF16)

    for copy in third:
        copy.wait()
    node_rows = slice(0, nodes)
    node_work[...] = flat_dot(node_x[...], node_in[...])
    for c in chunks(node_rows):
        value, node_slope[c, :] = silu_pair(node_work[c, :])
        node_act[c, :] = value.astype(BF16)
    node_work[...] = flat_dot(node_act[...], node_out[...])
    for c in chunks(node_rows):
        value, scale = layer_norm(node_work[c, :])
        node_new[c, :] = (node_x[c, 0:feat].astype(F32) + value).astype(BF16)
        up = node_cot[c, :].astype(F32)
        node_lin_grad[c, :] = norm_grad(value, scale, up).astype(BF16)
    stores.start(node_new, node_new_hbm)
    node_work[...] = outer_dot(node_lin_grad[...], node_out[...])
    for c in chunks(node_rows):
        node_pre_grad[c, :] = (node_work[c, :] * node_slope[c, :]).astype(BF16)
    node_work[...] = outer_dot(node_pre_grad[...], node_in[feat:, :])
    for c in chunks(node_rows):
        agg_parts[c, :], low_part = split_parts(node_work[c, :])
        agg_parts[slice(c.start + nodes, c.stop + nodes), :] = low_part
    stores.start(agg_parts, agg_parts_hbm)

    for copy in fourth:
        copy.wait()
    for rows in blocks:
        hot = receiver_hot[rows]
        edge_up[rows, :] = flat_dot(jnp.concatenate([hot, hot], 1), agg_parts[...])
        for c in chunks(rows):
            up = edge_cot[c, :].astype(F32) + edge_up[c, :]
            edge_up[c, :] = up
            lin_grad[c, :] = norm_grad(normed[c, :], inverse[c, :], up).astype(BF16)
        back_work[rows, :] = outer_dot(lin_grad[rows, :], edge_out[...])
        for c in chunks(rows):
            pre_grad[c, :] = (back_work[c, :] * slope[c, :]).astype(BF16)
    stores.start(pre_grad, pre_grad_hbm)
    taken = flat_dot(receiver_rows, pre_grad[...])

    def give(which, keep_ref, send_ref):
        order, low = places[which]
        half = keep_ref.shape[0] // (tiles // 2)
        if order is None:
            for upper in range(tiles // 2):
                to = pl.ds(upper * half, half)
                rows = slice(low, low + half)
                stores.start(weights.at[2 * upper + core, rows], keep_ref.at[to])
                stores.start(weights.at[2 * upper + 1 - core, rows], send_ref.at[to])
            return
        here = {"tile": tile, "dom": where_ref[3]}
        rows = keep_ref.shape[0] >> len(order)
        for index in range(1 << len(order)):
            upper = block = 0
            for at, (axis, bit) in enumerate(order):
                flipped = 1 - ((index >> (len(order) - 1 - at)) & 1)
                value = ((here[axis] >> bit) & 1) ^ flipped
                if axis == "tile":
                    upper = upper + (value << (bit - 1))
                else:
                    block = block + (value << bit)
            source = pl.ds(pl.multiple_of(low + block * rows, 16), rows)
            to = pl.ds(index * rows, rows)
            stores.start(weights.at[2 * upper + core, source], keep_ref.at[to])
            stores.start(weights.at[2 * upper + 1 - core, source], send_ref.at[to])

    part_rows = sums.shape[0] // 2
    for start in (0, part_rows):
        sums[start : start + part_rows, :] = flat_dot(
            hot_columns(sender[...], part_rows, start), pre_grad[...]
        )
    back_first_ref[...] = sums[pl.ds(part + turn, halo), :].astype(BF16)
    back_second_ref[...] = sums[pl.ds(part + halo - turn, halo), :].astype(BF16)
    for mask, ref, first in (
        (0, own_ref, 0),
        (2, opposite_ref, 0),
        (1, core_sums, 0),
        (3, core_sums, part),
    ):
        value = sums[rows_of(mask), :].astype(ref.dtype)
        for at in range(tiles):
            lanes = slice(at * width, (at + 1) * width)
            ref[first + at * nodes : first + (at + 1) * nodes, :] = value[:, lanes]
    stores.start(core_sums, send_upper_ref.at[pl.ds(send_lower_ref.shape[0], 2 * part)])
    put(weights, 4 * feat, inner_dot(node_x[...], node_pre_grad[...]))
    put(weights, 6 * feat, inner_dot(node_act[...], node_lin_grad[...]))
    put(weights, 3 * feat, inner_dot(act[...], lin_grad[...]))
    give(0, keep_upper_ref, send_upper_ref)
    high_part, low_part = split_parts(taken)
    put(weights, 2 * feat, inner_dot(latent, high_part) + inner_dot(latent, low_part))
    put(weights, feat, inner_dot(picked[...], pre_grad[...]))
    for copy in fifth:
        copy.wait()
    put(weights, 0, flat_dot(edge_t[...], pre_grad[...]))
    give(1, keep_lower_ref, send_lower_ref)
    local_ref[...] = (
        node_cot[...].astype(F32)
        + outer_dot(node_pre_grad[...], node_in[0:feat, :])
        + (outer_dot(high_part, w_recv[...]) + outer_dot(low_part, w_recv[...]))
    )
    stores.finish()


def edge_grad_kernel(
    receiver_hbm,
    pre_grad_hbm,
    edge_cot_hbm,
    w_hbm,
    agg_parts_hbm,
    out_hbm,
    receiver,
    pre_grad,
    edge_cot,
    w_edge,
    agg_parts,
    work,
    out,
    in_sems,
    out_sems,
):
    loads, stores = Copies(in_sems), Copies(out_sems)
    for source, target in (
        (receiver_hbm, receiver),
        (agg_parts_hbm, agg_parts),
        (w_hbm.at[0 : w_edge.shape[0]], w_edge),
        (pre_grad_hbm, pre_grad),
        (edge_cot_hbm, edge_cot),
    ):
        loads.start(source, target)
    loads.finish()
    column = as_column(receiver[...])
    for at in range(0, out.shape[0], ROWS):
        rows = slice(at, at + ROWS)
        hot = hot_rows(column[rows], agg_parts.shape[0] // 2)
        work[rows, :] = flat_dot(jnp.concatenate([hot, hot], 1), agg_parts[...]) + outer_dot(
            pre_grad[rows, :], w_edge[...]
        )
        for start in range(at, at + ROWS, CHUNK):
            c = slice(start, start + CHUNK)
            out[c, :] = (edge_cot[c, :].astype(F32) + work[c, :]).astype(BF16)
        stores.start(out.at[rows], out_hbm.at[rows])
    stores.finish()


def node_kernel(
    where_ref,
    from_ref,
    cut_ref,
    w_send_ref,
    local_ref,
    total_ref,
    first_ref,
    second_ref,
    stay_ref,
    slot_ref,
    ends,
):
    nodes, feat = local_ref.shape
    halo = first_ref.shape[0]
    width = total_ref.shape[1]
    turn = pl.multiple_of(where_ref[2], halo)
    ends[pl.ds(turn, halo), :] = first_ref[...]
    ends[pl.ds(halo - turn, halo), :] = second_ref[...]
    value = jnp.concatenate(
        [total_ref[block * nodes : (block + 1) * nodes, :] for block in range(feat // width)], 1
    )
    value = value + flat_dot(hot_columns(cut_ref[...], nodes), ends[...])
    high_part, low_part = split_parts(value)
    w_send = w_send_ref[...]
    grad = local_ref[...] + (outer_dot(high_part, w_send) + outer_dot(low_part, w_send))
    grad = grad.astype(BF16)
    where = from_ref[...]
    slot_ref[...] = flat_dot(hot_columns(where, slot_ref.shape[0], nodes), grad).astype(BF16)
    stay_ref[...] = flat_dot(hot_columns(where, nodes), grad).astype(BF16)


def back_kernel(pick_ref, stay_ref, came_ref, out_hbm, out, out_sems):
    stores = Copies(out_sems)
    hot = hot_columns(pick_ref[...], stay_ref.shape[0])
    out[...] = (stay_ref[...].astype(F32) + flat_dot(hot, came_ref[...])).astype(BF16)
    stores.start(out, out_hbm)
    stores.finish()


def flip(values, axis, mask):
    count = lax.axis_size(axis)
    return lax.ppermute(values, axis, [(i, i ^ mask) for i in range(count)])


def meet(values, axis, step):
    count = lax.axis_size(axis)
    pairs = [(i, (i + (step if i % 2 == 0 else -step)) % count) for i in range(count)]
    return lax.ppermute(values, axis, pairs)


def axis_bits(axis):
    return [(axis, b) for b in range(lax.axis_size(axis).bit_length() - 1)]


def exchange_orders():
    cross, dom_bits = axis_bits("tile")[1:], axis_bits("dom")
    side, line = dom_bits[:1], dom_bits[1:-1]
    return side + cross + line, line + side + cross


def after(values, *others):
    return lax.optimization_barrier((values, others))[0]


def total_of(values):
    return functools.reduce(jnp.add, [v.astype(F32) for v in values])


class Exchange:
    def __init__(self, values, count, order, relative):
        self.values = values
        self.count = count
        self.order = list(order)
        self.relative = relative
        self.outgoing = None

    def cut(self, *others):
        arrays = after(self.values, *others)
        self.count //= 2
        axis, bit = self.order[0]
        mine = (lax.axis_index(axis) >> bit) & 1

        def half(second):
            if self.relative:
                first = int(second) * self.count
                return total_of([a[first : first + self.count] for a in arrays]).astype(BF16)
            first = (mine if second else 1 - mine) * self.count
            return total_of(
                [lax.dynamic_slice_in_dim(a, first, self.count, 0) for a in arrays]
            ).astype(BF16)

        self.outgoing = half(False)
        self.values = [half(True)]
        return self.outgoing

    def send(self):
        axis, bit = self.order.pop(0)
        self.values.append(flip(self.outgoing, axis, 1 << bit))

    def total(self):
        return total_of(self.values)


def cut_all(parts, *others):
    return [part.cut(*others) for part in parts]


def send_all(parts):
    for part in parts:
        part.send()


def body(
    tile_latent,
    relay_pick,
    relay_from,
    cut_pick,
    edge_latent,
    edge_sender,
    edge_receiver,
    edge_in,
    edge_out,
    node_in,
    node_out,
    node_cot,
    edge_cot,
):
    nodes, feat = tile_latent.shape
    edges = edge_latent.shape[0]
    doms, tiles = lax.axis_size("dom"), lax.axis_size("tile")
    slots = relay_pick.shape[1]
    halo = cut_pick.shape[1] // 2
    table_rows = -(-(tiles * nodes + 2 * halo) // nodes) * nodes
    half, width = 7 * feat // 2, feat // tiles
    sds = jax.ShapeDtypeStruct
    node_bf16 = sds((nodes, feat), BF16)
    node_f32 = sds((nodes, feat), F32)
    edge_bf16 = sds((edges, feat), BF16)
    edge_f32 = sds((edges, feat), F32)
    slot_bf16 = sds((slots, feat), BF16)
    halo_bf16 = sds((halo, feat), BF16)
    square = sds((feat, feat), BF16)
    node_index = sds((nodes,), jnp.int32)
    edge_index = sds((edges,), jnp.int32)

    def exchange(rows):
        blocks = rows.reshape(doms, slots // doms, feat)
        return lax.all_to_all(blocks, "dom", split_axis=0, concat_axis=0, tiled=True).reshape(
            slots, feat
        )

    tile = lax.axis_index("tile")
    turn = jnp.where(lax.axis_index("dom") % 2 == 0, halo, 0)
    where = jnp.stack([tile & 1, tile, turn, lax.axis_index("dom")]).astype(jnp.int32)
    outgoing, pick_row, tile_rows, from_row, cut_row = call(
        pick_kernel,
        "pick",
        [Kept(slot_bf16), Kept(relay_pick), Kept(node_bf16)]
        + [Kept(sds((1, nodes), jnp.int32)), Kept(cut_pick)],
        [relay_pick, tile_latent, relay_from, cut_pick],
        [node_index, 4],
        limit=SMALL_LIMIT,
    )
    edge_t = jnp.transpose(after(edge_latent, outgoing))
    came = after(exchange(outgoing), edge_t)
    latent, first, second = call(
        pool_kernel,
        "pool",
        [Kept(node_bf16), Kept(halo_bf16), Kept(halo_bf16)],
        [Kept(array) for array in (from_row, cut_row, tile_rows, came)],
        [sds((2 * halo, feat), BF16)],
        [where],
        SMALL_LIMIT,
    )
    far = flip(latent, "tile", 2)
    near = flip(latent, "tile", 1)
    first = meet(first, "dom", 1)
    second = meet(second, "dom", -1)
    base, w_send, w_out = call(
        base_kernel,
        "base",
        [Kept(edge_f32), Kept(square), Kept(square)],
        [edge_receiver, edge_latent, edge_in, edge_out, Kept(latent)],
        [edge_index, edge_bf16, square, square, 6],
    )
    across = flip(after(far, first, second, base), "tile", 1)

    orders = exchange_orders()
    rows = 7 * feat // doms
    bits = len(orders[0])
    fine = rows % 16 == 0
    span = tiles * half // 2
    places = [(order if fine else None, low) for order, low in zip(orders, (half, 0))]
    copies = 2 * sum(1 << len(order) if fine else tiles // 2 for order in orders)
    sum_rows = tiles * nodes
    (
        node_new,
        edge_new,
        pre_grad,
        agg_parts,
        local,
        keep_upper,
        keep_lower,
        send_upper,
        send_lower,
        own,
        opposite,
        back_first,
        back_second,
    ) = call(
        functools.partial(block_kernel, places),
        "block",
        [node_bf16, edge_bf16, edge_bf16, sds((2 * nodes, feat), BF16), Kept(node_f32)]
        + [sds((span, width), BF16)] * 2
        + [sds((span + 2 * sum_rows, width), BF16), sds((span, width), BF16)]
        + [Kept(sds((sum_rows, width), F32)), Kept(sds((sum_rows, width), BF16))]
        + [Kept(halo_bf16)] * 2,
        [edge_sender, edge_receiver]
        + [Kept(array) for array in (latent, near, far, across, first, second)]
        + [Kept(base), Kept(w_send), Kept(w_out)]
        + [edge_latent, edge_t, edge_in, node_in, node_out, node_cot, edge_cot],
        [edge_index, edge_index, sds((table_rows, feat), BF16), edge_bf16]
        + [sds((feat, edges), BF16), edge_bf16, square, sds((nodes, 2 * feat), BF16)]
        + [node_in, node_out, node_cot, edge_cot]
        + [node_bf16] * 4
        + [sds((2 * nodes, feat), BF16), node_f32, node_f32]
        + [edge_bf16] * 4
        + [edge_f32] * 3
        + [sds((edges, 1), F32), edge_f32, edge_f32]
        + [sds((tiles, 2 * half, width), BF16), sds((table_rows, feat), F32)]
        + [sds((2 * sum_rows, width), BF16)]
        + [9, 5 + copies],
        [where],
    )
    got_upper = flip(send_upper, "tile", 1)
    got_lower = flip(send_lower, "tile", 1)
    back_first = meet(back_first, "dom", 1)
    back_second = meet(back_second, "dom", -1)
    leaving = (opposite.astype(F32) + got_upper[span + sum_rows :].astype(F32)).astype(BF16)
    across = flip(leaving, "tile", 2)
    parts = []
    for order, keep, got in zip(
        orders, (keep_upper, keep_lower), (got_upper, got_lower), strict=True
    ):
        if fine:
            parts.append(Exchange([keep, got], span, order, True))
            continue
        labels = axis_bits("tile")[:0:-1] + axis_bits("dom")[-2::-1]
        axes = [labels.index(label) for label in order] + [bits, bits + 1]
        values = [
            jnp.transpose(whole.reshape([2] * bits + [rows, width]), axes)
            for whole in (keep, got[:span])
        ]
        parts.append(Exchange([v.reshape(span, width) for v in values], span, order, False))
    sent = parts[0].cut()
    parts[0].send()
    sent = parts[1].cut(sent, back_first, back_second)
    parts[1].send()
    total = own + got_upper[span : span + sum_rows].astype(F32) + across.astype(F32)
    stay, slot_grad = call(
        node_kernel,
        "node",
        [Kept(node_bf16), Kept(slot_bf16)],
        [Kept(array) for array in (from_row, cut_row, w_send, after(local, sent), total)]
        + [Kept(back_first), Kept(back_second)],
        [sds((2 * halo, feat), BF16)],
        [where],
        SMALL_LIMIT,
    )
    back_rows = exchange(slot_grad)
    sent = cut_all(parts, slot_grad)
    send_all(parts)
    [latent_grad] = call(
        back_kernel,
        "back",
        [node_bf16],
        [Kept(pick_row), Kept(stay), Kept(after(back_rows, *sent))],
        [node_bf16, 1],
        limit=SMALL_LIMIT,
    )
    first = latent_grad
    while parts[0].order:
        sent = cut_all(parts, first)
        send_all(parts)
        first = ()
    [edge_grad] = call(
        edge_grad_kernel,
        "edge_grad",
        [edge_bf16],
        [edge_receiver, after(pre_grad, *sent), edge_cot, edge_in, agg_parts],
        [edge_index, edge_bf16, edge_bf16, square, sds((2 * nodes, feat), BF16)]
        + [edge_f32, edge_bf16, 5, edges // ROWS],
        limit=2 * SMALL_LIMIT,
    )
    for part in parts:
        part.values = after(part.values, edge_grad)
    top = axis_bits("dom")[-1][1]
    upper = (lax.axis_index("dom") >> top) & 1
    above, below = [part.total() for part in parts]
    sent = jnp.where(upper == 1, below, above).astype(BF16)
    kept = jnp.where(upper == 1, above, below)
    weight_shard = kept + flip(sent, "dom", 1 << top).astype(F32)
    return (node_new, edge_new, latent_grad, edge_grad, weight_shard)


def solution(mesh):
    rows = P(("dom", "tile"), None)
    flat = P(("dom", "tile"))
    in_specs = (rows, rows, flat, rows, rows, flat, flat, P(), P(), P(), P(), rows, rows)
    out_specs = (rows, rows, rows, rows, P("dom", "tile"))
    return jax.shard_map(body, mesh=mesh, in_specs=in_specs, out_specs=out_specs, check_vma=False)
```
